32 devices in a mesh: pipe: 2 (over x), expert: 8 (over z, y), tensor: 2 (over core).
Axes of the slice: x: 2, y: 2, z: 4, core: 2. Of those that a mesh axis runs over, the one named last changes fastest.
Arguments:
- tokens: bfloat16 [2048, 6144], P(('pipe', 'expert'), 'tensor'), parts along dimension 0, may hold values from -6 to 6
- grad_out: bfloat16 [2048, 6144], P(('pipe', 'expert'), 'tensor'), parts along dimension 0, may hold values from -6 to 6
- expert_ids: int32 [2048, 2], P(('pipe', 'expert')), parts along dimension 0, may hold values from 0 to 7, all different within a row; in each aligned block of 128 rows (0 to 127, 128 to 255, ...) at most 36 rows name the same one
- gate_probs: float32 [2048, 2], P(('pipe', 'expert')), parts along dimension 0, may hold values from 0.05 to 1
- w_gate: bfloat16 [6144, 2048], P('tensor', 'expert'), may hold values from -0.078125 to 0.078125
- w_up: bfloat16 [6144, 2048], P('tensor', 'expert'), may hold values from -0.078125 to 0.078125
- w_down: bfloat16 [2048, 6144], P('expert', 'tensor'), may hold values from -0.078125 to 0.078125
Outputs:
- grad_in: bfloat16 [2048, 6144], P(('pipe', 'expert'), 'tensor'), parts along dimension 0
- grad_gate: bfloat16 [12288, 2048], P(('pipe', 'tensor'), 'expert'), parts along dimension 0
- grad_up: bfloat16 [12288, 2048], P(('pipe', 'tensor'), 'expert'), parts along dimension 0
- grad_down: bfloat16 [4096, 6144], P(('pipe', 'expert'), 'tensor'), parts along dimension 0
The draws below stay inside these ranges and needn't reach their ends.
There are 2 independent parts, one for each index of `pipe`. The reference program is written for one: setup_inputs(seed, part) draws one part's arguments, and reference() takes and returns one part's arrays. A program takes and returns all parts, laid end to end along the dimension named above; an argument that names none is the same for every part. Nothing has to cross between parts.
Inputs may be any that keep to these rules, and one draw needn't show every extreme that they name: `expert_ids`: each token names two different experts. In the rows of one device no expert is named by more than 36 tokens, a bound that some block reaches of them.
All inputs are finite; a program needn't handle non-finite values.
Results may differ from the reference program's by a relative error of at most 0.02.
Values may be sent and summed in bfloat16 or wider, within the bound.
No kernel may reach another device: no remote copies, remote signals or barrier semaphores. Data moves between devices by JAX's collectives and lax.ppermute only.
A program may use at most 128 MiB of HBM per device.

```python
import math
import jax
import jax.numpy as jnp
import numpy as np
from jax import lax

D = 6144
EXPERTS = 8
F_DEV = 256
TOK_DEV = 128
CAP = 36
HIDDEN_SIZE = 2048
TOKENS = 1024


def levels(stream_key, extent, cuts, smallest, high):
    level = 1.0
    for axis_at, blocks in cuts:
        draws = jax.random.uniform(jax.random.fold_in(jax.random.fold_in(stream_key, 6), axis_at), (blocks,), jnp.float32, smallest / len(cuts), high / len(cuts))
        level = level * jnp.repeat(jnp.exp(draws), extent[axis_at] // blocks).reshape((-1,) + (1,) * (len(extent) - 1 - axis_at))
    return level


def deal_out(key, own, number, rows, count, top, bound, skew):
    sequence = jax.random.permutation(key, count)
    crowded, usual = portions_of(count, rows * top, bound, skew, True), portions_of(count, rows * top, bound, skew, False)
    places = jnp.arange(count)

    def named(tallies, offset_by):
        used = int((tallies > 0).sum())
        fixed = max(1, used // 4)
        shifted = fixed + (places - fixed + offset_by * (used - fixed)) % max(1, count - fixed)
        return jnp.zeros((count,), jnp.int32).at[sequence[jnp.where(places < fixed, places, shifted)]].set(jnp.asarray(tallies, jnp.int32))

    tallies = jnp.where(number % 4 == 0, named(crowded, number // 4), named(usual, number - number // 4 - 1))
    mixed = jax.random.permutation(jax.random.fold_in(own, 3), count)
    donor, sink = mixed[0:count // 2 * 2:2], mixed[1:count // 2 * 2:2]
    margin = jnp.minimum(tallies[donor] - 1, bound - tallies[sink]) // 2
    margin = jnp.where((donor == sequence[0]) | (sink == sequence[0]) | (tallies[sink] == 0), 0, jnp.maximum(margin, 0))
    shifted = jax.random.randint(jax.random.fold_in(own, 4), (count // 2,), 0, 1 << 20) % (margin + 1)
    tallies = tallies.at[donor].add(-shifted).at[sink].add(shifted)
    labels = jnp.searchsorted(jnp.cumsum(tallies), jnp.arange(rows * top), side="right").astype(jnp.int32)
    grid = labels.reshape(top, rows).T
    grid = grid[jax.random.permutation(jax.random.fold_in(own, 1), rows)]
    offset_by = jax.random.randint(jax.random.fold_in(own, 2), (rows, 1), 0, top)
    return jnp.take_along_axis(grid, (jnp.arange(top)[None, :] + offset_by) % top, axis=1)


def portions_of(number_of, total, most, slope, full):
    portions = [(1 << 20) // math.isqrt(grade ** slope) + 1 for grade in range(1, number_of + 1)]
    largest = most if full else min(most, max(-(-total // number_of), total * portions[0] // sum(portions)))
    least = 1 if total - largest >= number_of - 1 else 0
    holding, rest = [largest] + [least] * (number_of - 1), total - largest - least * (number_of - 1)
    while rest > 0:
        free = [i for i in range(1, number_of) if holding[i] < largest] or [i for i in range(1, number_of) if holding[i] < most]
        mass, remaining = sum([portions[i] for i in free]), rest
        for i in free:
            addition = min(most - holding[i], max(1, remaining * portions[i] // mass), rest)
            holding[i] = holding[i] + addition
            rest = rest - addition
    return np.array(holding)


def scatter_about(key, dims, scale, bound, shards=(), kind=jnp.bfloat16):
    array = scale * jax.random.normal(key, dims, jnp.float32)
    if shards:
        array = array * levels(key, dims, shards, -0.22, 0.18)
    return jnp.clip(array, -bound, bound).astype(kind)


def setup_inputs(seed: int = 0, part: int = 0) -> dict:
    seeds = jax.random.split(jax.random.key(seed), 8)
    own_keys = jax.random.split(jax.random.fold_in(seeds[7], part), 8)
    tokens = scatter_about(own_keys[0], (TOKENS, D), 1.0, 6.0, ((0, 8), (1, 2)))
    grad_out = scatter_about(own_keys[1], (TOKENS, D), 1.0, 6.0, ((0, 8), (1, 2)))
    expert_ids_keys = jax.random.split(jax.random.fold_in(own_keys[2], 1), TOKENS // TOK_DEV)
    expert_ids_turns = jax.random.permutation(jax.random.fold_in(own_keys[2], 3), TOKENS // TOK_DEV)
    expert_ids = jax.vmap(lambda own, number: deal_out(jax.random.fold_in(own_keys[2], 2), own, number, TOK_DEV, EXPERTS, 2, CAP, 0))(expert_ids_keys, expert_ids_turns).reshape((TOKENS, 2))
    gate_probs = jnp.clip(jnp.exp(math.log(1.0) - 2.9957323 * jax.random.uniform(own_keys[3], (TOKENS, 2), jnp.float32) ** levels(own_keys[3], (TOKENS, 2), ((0, 8),), -0.2, 0.2)), 0.05, 1.0)
    w_gate = scatter_about(seeds[4], (D, HIDDEN_SIZE), D ** -0.5, 0.078125, ((0, 2), (1, 8)))
    w_up = scatter_about(seeds[5], (D, HIDDEN_SIZE), D ** -0.5, 0.078125, ((0, 2), (1, 8)))
    w_down = scatter_about(seeds[6], (HIDDEN_SIZE, D), D ** -0.5, 0.078125, ((0, 8), (1, 2)))
    return dict(tokens=tokens, grad_out=grad_out, expert_ids=expert_ids, gate_probs=gate_probs, w_gate=w_gate, w_up=w_up, w_down=w_down)


window_expert = 0


def swiglu_grads(sums, width):
    z_gate = sums[:, :width]
    z_up = sums[:, width:2 * width]
    d_hidden = sums[:, 2 * width:]
    sig = jax.nn.sigmoid(z_gate)
    act = z_gate * sig
    hidden = (act * z_up).astype(jnp.bfloat16)
    d_gate = (d_hidden * z_up * sig * (1.0 + z_gate * (1.0 - sig))).astype(jnp.bfloat16)
    d_up = (d_hidden * act).astype(jnp.bfloat16)
    return hidden, jnp.concatenate([d_gate, d_up], axis=1)


def reference(tokens, grad_out, expert_ids, gate_probs, w_gate, w_up, w_down):
    chosen = expert_ids == window_expert
    weight = jnp.sum(jnp.where(chosen, gate_probs, jnp.zeros_like(gate_probs)), axis=1)
    scaled = (weight[:, None] * grad_out.astype(jnp.float32)).astype(jnp.bfloat16)
    w_in = jnp.concatenate([w_gate, w_up], axis=1)
    front = jnp.dot(tokens, w_in, preferred_element_type=jnp.float32)
    back = jnp.dot(scaled, w_down.T, preferred_element_type=jnp.float32)
    hidden, d_pre = swiglu_grads(jnp.concatenate([front, back], axis=1), HIDDEN_SIZE)

    def add_block(total, index):
        low = (index * F_DEV).astype(jnp.int32)
        d_gate = lax.dynamic_slice_in_dim(d_pre, low, F_DEV, 1)
        d_up = lax.dynamic_slice_in_dim(d_pre, (low + HIDDEN_SIZE).astype(jnp.int32), F_DEV, 1)
        gate_cols = lax.dynamic_slice_in_dim(w_gate, low, F_DEV, 1)
        up_cols = lax.dynamic_slice_in_dim(w_up, low, F_DEV, 1)
        term = jnp.dot(d_gate, gate_cols.T, preferred_element_type=jnp.float32)
        term = term + jnp.dot(d_up, up_cols.T, preferred_element_type=jnp.float32)
        rounded = lax.optimization_barrier(term.astype(jnp.bfloat16))
        return total + rounded.astype(jnp.float32), None

    start = jnp.zeros((tokens.shape[0], tokens.shape[1]), jnp.float32)
    total, _ = lax.scan(add_block, start, jnp.arange(HIDDEN_SIZE // F_DEV, dtype=jnp.int32))
    grad_in = total.astype(jnp.bfloat16)
    grad_w_in = jnp.dot(tokens.T, d_pre, preferred_element_type=jnp.float32).astype(jnp.bfloat16)
    grad_down = jnp.dot(hidden.T, scaled, preferred_element_type=jnp.float32).astype(jnp.bfloat16)
    return grad_in, grad_w_in[:, :HIDDEN_SIZE], grad_w_in[:, HIDDEN_SIZE:], grad_down
```

```python
import jax
import jax.numpy as jnp
from jax import lax
from jax.sharding import PartitionSpec as P

CAP = 36


window_expert = 0


def swiglu_grads(sums, width):
    z_gate = sums[:, :width]
    z_up = sums[:, width : 2 * width]
    d_hidden = sums[:, 2 * width :]
    sig = jax.nn.sigmoid(z_gate)
    act = z_gate * sig
    hidden = (act * z_up).astype(jnp.bfloat16)
    d_gate = (d_hidden * z_up * sig * (1.0 + z_gate * (1.0 - sig))).astype(jnp.bfloat16)
    d_up = (d_hidden * act).astype(jnp.bfloat16)
    return (hidden, jnp.concatenate([d_gate, d_up], axis=1))


def place(tokens, grad_out, expert_ids, gate_probs):
    chosen = expert_ids == window_expert
    weight = jnp.sum(jnp.where(chosen, gate_probs, jnp.zeros_like(gate_probs)), axis=1)
    scaled = (weight[:, None] * grad_out.astype(jnp.float32)).astype(jnp.bfloat16)
    routed = jnp.any(chosen, axis=1)
    slot_of = jnp.cumsum(routed.astype(jnp.int32)) - 1
    slot_ids = jnp.arange(CAP, dtype=jnp.int32)
    placing = ((slot_of[None, :] == slot_ids[:, None]) & routed[None, :]).astype(jnp.bfloat16)
    send_x = jnp.dot(placing, tokens, preferred_element_type=jnp.float32).astype(jnp.bfloat16)
    send_dy = jnp.dot(placing, scaled, preferred_element_type=jnp.float32).astype(jnp.bfloat16)
    return placing, send_x, send_dy


def unplace(placing, summed):
    return lax.dot_general(
        placing, summed, (((0,), (0,)), ((), ())), preferred_element_type=jnp.float32
    ).astype(jnp.bfloat16)


def weight_grads(rows_x, rows_dy, hidden, d_pre, width):
    grad_w_in = lax.dot_general(
        rows_x, d_pre, (((0,), (0,)), ((), ())), preferred_element_type=jnp.float32
    ).astype(jnp.bfloat16)
    grad_down = lax.dot_general(
        hidden, rows_dy, (((0,), (0,)), ((), ())), preferred_element_type=jnp.float32
    ).astype(jnp.bfloat16)
    return (grad_w_in[:, :width], grad_w_in[:, width:], grad_down)


def any_size(tokens, grad_out, expert_ids, gate_probs, w_gate, w_up, w_down):
    width = w_gate.shape[1]
    placing, send_x, send_dy = place(tokens, grad_out, expert_ids, gate_probs)
    rows_x, rows_dy = (
        lax.all_gather(send_x, "expert", axis=0, tiled=True),
        lax.all_gather(send_dy, "expert", axis=0, tiled=True),
    )
    w_in = jnp.concatenate([w_gate, w_up], axis=1)
    front = jnp.dot(rows_x, w_in, preferred_element_type=jnp.float32)
    back = lax.dot_general(
        rows_dy, w_down, (((1,), (1,)), ((), ())), preferred_element_type=jnp.float32
    )
    partial_value = jnp.concatenate([front, back], axis=1)
    share = lax.psum_scatter(
        partial_value.astype(jnp.bfloat16), "tensor", scatter_dimension=0, tiled=True
    ).astype(jnp.float32)
    hidden_part, grads_part = swiglu_grads(share, width)
    hidden, d_pre = (
        lax.all_gather(hidden_part, "tensor", axis=0, tiled=True),
        lax.all_gather(grads_part, "tensor", axis=0, tiled=True),
    )
    summed = lax.psum_scatter(
        lax.dot_general(
            d_pre, w_in, (((1,), (1,)), ((), ())), preferred_element_type=jnp.float32
        ).astype(jnp.bfloat16),
        "expert",
        scatter_dimension=0,
        tiled=True,
    )
    grad_in = unplace(placing, summed)
    return (grad_in,) + weight_grads(rows_x, rows_dy, hidden, d_pre, width)


def four_by_two(tokens, grad_out, expert_ids, gate_probs, w_gate, w_up, w_down):
    width = w_gate.shape[1]
    bf16, f32 = jnp.bfloat16, jnp.float32
    line = lax.axis_index("expert") // 2
    inner = (line == 1) | (line == 2)

    def send(value, pairs):
        return lax.ppermute(value, "expert", pairs)

    def across(value):
        return send(value, [(i, i ^ 1) for i in range(8)])

    def along(value, distance):
        return send(value, [(i, i ^ (2 * distance)) for i in range(8)])

    placing, send_x, send_dy = place(tokens, grad_out, expert_ids, gate_probs)
    own = jnp.concatenate([send_x, send_dy], axis=0)

    own_y = across(own)
    two = along(own, 2)
    one = along(own, 1)
    middle = send(own, [(2, 4), (3, 5), (4, 2), (5, 3)])
    ends = send(two, [(4, 6), (5, 7), (2, 0), (3, 1)])
    one_y = across(one)
    two_y = across(two)
    three = jnp.where(inner, middle, ends)
    three_y = across(three)

    w_in = jnp.concatenate([w_gate, w_up], axis=1)

    def group(mine, other):
        rows_x = jnp.concatenate([mine[:CAP], other[:CAP]], axis=0)
        rows_dy = jnp.concatenate([mine[CAP:], other[CAP:]], axis=0)
        front = jnp.dot(rows_x, w_in, preferred_element_type=f32)
        back = lax.dot_general(
            rows_dy, w_down, (((1,), (1,)), ((), ())), preferred_element_type=f32
        )
        part = jnp.concatenate([front, back], axis=1)
        sums = part + lax.ppermute(part.astype(bf16), "tensor", [(0, 1), (1, 0)]).astype(f32)
        hidden, d_pre = swiglu_grads(sums, width)
        term = lax.dot_general(
            d_pre, w_in, (((1,), (1,)), ((), ())), preferred_element_type=f32
        )
        arrived = across(term[CAP:].astype(bf16))
        return rows_x, rows_dy, hidden, d_pre, term[:CAP] + arrived.astype(f32)

    groups = [group(own, own_y), group(one, one_y), group(two, two_y), group(three, three_y)]
    total = groups[0][4]
    for distance in (1, 2, 3):
        total = total + along(groups[distance][4].astype(bf16), distance).astype(f32)
    grad_in = unplace(placing, total.astype(bf16))
    rows_x, rows_dy, hidden, d_pre = (
        jnp.concatenate([g[i] for g in groups], axis=0) for i in range(4)
    )
    return (grad_in,) + weight_grads(rows_x, rows_dy, hidden, d_pre, width)


def solution(mesh):
    in_specs = (
        P(("pipe", "expert"), "tensor"),
        P(("pipe", "expert"), "tensor"),
        P(("pipe", "expert"), None),
        P(("pipe", "expert"), None),
        P("tensor", "expert"),
        P("tensor", "expert"),
        P("expert", "tensor"),
    )
    out_specs = (
        P(("pipe", "expert"), "tensor"),
        P(("pipe", "tensor"), "expert"),
        P(("pipe", "tensor"), "expert"),
        P(("pipe", "expert"), "tensor"),
    )
    body = four_by_two if mesh.shape["expert"] == 8 and mesh.shape["tensor"] == 2 else any_size
    return jax.shard_map(body, mesh=mesh, in_specs=in_specs, out_specs=out_specs, check_vma=False)
```

```python
import jax
import jax.numpy as jnp
from jax import lax
from jax.experimental import pallas as pl
from jax.experimental.pallas import tpu as pltpu
from jax.sharding import PartitionSpec as P

CAP = 36


window_expert = 0


def swiglu_grads(sums, width):
    z_gate = sums[:, :width]
    z_up = sums[:, width : 2 * width]
    d_hidden = sums[:, 2 * width :]
    sig = jax.nn.sigmoid(z_gate)
    act = z_gate * sig
    hidden = (act * z_up).astype(jnp.bfloat16)
    d_gate = (d_hidden * z_up * sig * (1.0 + z_gate * (1.0 - sig))).astype(jnp.bfloat16)
    d_up = (d_hidden * act).astype(jnp.bfloat16)
    return (hidden, jnp.concatenate([d_gate, d_up], axis=1))


def place(tokens, grad_out, expert_ids, gate_probs):
    chosen = expert_ids == window_expert
    weight = jnp.sum(jnp.where(chosen, gate_probs, jnp.zeros_like(gate_probs)), axis=1)
    scaled = (weight[:, None] * grad_out.astype(jnp.float32)).astype(jnp.bfloat16)
    routed = jnp.any(chosen, axis=1)
    slot_of = jnp.cumsum(routed.astype(jnp.int32)) - 1
    slot_ids = jnp.arange(CAP, dtype=jnp.int32)
    placing = ((slot_of[None, :] == slot_ids[:, None]) & routed[None, :]).astype(jnp.bfloat16)
    send_x = jnp.dot(placing, tokens, preferred_element_type=jnp.float32).astype(jnp.bfloat16)
    send_dy = jnp.dot(placing, scaled, preferred_element_type=jnp.float32).astype(jnp.bfloat16)
    return placing, send_x, send_dy


def unplace(placing, summed):
    return lax.dot_general(
        placing, summed, (((0,), (0,)), ((), ())), preferred_element_type=jnp.float32
    ).astype(jnp.bfloat16)


def weight_grads(rows_x, rows_dy, hidden, d_pre, width):
    grad_w_in = lax.dot_general(
        rows_x, d_pre, (((0,), (0,)), ((), ())), preferred_element_type=jnp.float32
    ).astype(jnp.bfloat16)
    grad_down = lax.dot_general(
        hidden, rows_dy, (((0,), (0,)), ((), ())), preferred_element_type=jnp.float32
    ).astype(jnp.bfloat16)
    return (grad_w_in[:, :width], grad_w_in[:, width:], grad_down)


def any_size(tokens, grad_out, expert_ids, gate_probs, w_gate, w_up, w_down):
    width = w_gate.shape[1]
    placing, send_x, send_dy = place(tokens, grad_out, expert_ids, gate_probs)
    rows_x, rows_dy = (
        lax.all_gather(send_x, "expert", axis=0, tiled=True),
        lax.all_gather(send_dy, "expert", axis=0, tiled=True),
    )
    w_in = jnp.concatenate([w_gate, w_up], axis=1)
    front = jnp.dot(rows_x, w_in, preferred_element_type=jnp.float32)
    back = lax.dot_general(
        rows_dy, w_down, (((1,), (1,)), ((), ())), preferred_element_type=jnp.float32
    )
    partial_value = jnp.concatenate([front, back], axis=1)
    share = lax.psum_scatter(
        partial_value.astype(jnp.bfloat16), "tensor", scatter_dimension=0, tiled=True
    ).astype(jnp.float32)
    hidden_part, grads_part = swiglu_grads(share, width)
    hidden, d_pre = (
        lax.all_gather(hidden_part, "tensor", axis=0, tiled=True),
        lax.all_gather(grads_part, "tensor", axis=0, tiled=True),
    )
    summed = lax.psum_scatter(
        lax.dot_general(
            d_pre, w_in, (((1,), (1,)), ((), ())), preferred_element_type=jnp.float32
        ).astype(jnp.bfloat16),
        "expert",
        scatter_dimension=0,
        tiled=True,
    )
    grad_in = unplace(placing, summed)
    return (grad_in,) + weight_grads(rows_x, rows_dy, hidden, d_pre, width)


MAIN = 32
TAIL = CAP - MAIN
BLOCK = 2 * CAP
TERM = 40
GROUP = 80
BF16, F32 = jnp.bfloat16, jnp.float32


def struct(rows, columns, dtype):
    return jax.ShapeDtypeStruct((rows, columns), dtype)


def call(kernel, outs, *args, name, **more):
    return pl.pallas_call(
        kernel,
        out_shape=outs,
        name=name,
        compiler_params=pltpu.CompilerParams(vmem_limit_bytes=24 * 2**20),
        cost_estimate=pl.CostEstimate(flops=1000, bytes_accessed=1000, transcendentals=0),
        **more,
    )(*args)


def mul(left, right, left_dim=1, right_dim=0):
    return lax.dot_general(
        left, right, (((left_dim,), (right_dim,)), ((), ())), preferred_element_type=F32
    )


def place_kernel(tokens, grad_out, ids, probs, block, placing_t):
    rows = tokens.shape[0]
    chosen = ids[...] == window_expert
    weight = jnp.sum(jnp.where(chosen, probs[...], 0.0), axis=1, keepdims=True)
    routed = jnp.max(chosen.astype(F32), axis=1, keepdims=True)
    at_row = lax.broadcasted_iota(jnp.int32, (rows, rows), 0)
    at_column = lax.broadcasted_iota(jnp.int32, (rows, rows), 1)
    same = at_row == at_column
    routed_row = jnp.sum(jnp.where(same, routed, 0.0), axis=0, keepdims=True)
    weight_row = jnp.sum(jnp.where(same, weight, 0.0), axis=0, keepdims=True)
    slot_row = jnp.sum(jnp.where(at_row <= at_column, routed, 0.0), axis=0, keepdims=True) - 1.0
    slot = jnp.sum(jnp.where(at_column <= at_row, routed_row, 0.0), axis=1, keepdims=True) - 1.0
    wanted = lax.broadcasted_iota(jnp.int32, (TERM, rows), 0).astype(F32)
    placing = jnp.where((slot_row == wanted) & (routed_row > 0.0), 1.0, 0.0)
    wanted = at_column.astype(F32)
    placing_t[...] = jnp.where((slot == wanted) & (routed > 0.0), 1.0, 0.0).astype(BF16)
    scale = jnp.sum(placing * weight_row, axis=1, keepdims=True)
    placing = placing.astype(BF16)
    x = mul(placing, tokens[...])
    dy = mul(placing, grad_out[...]) * scale
    block[0:MAIN, :] = x[0:MAIN].astype(BF16)
    block[MAIN : 2 * MAIN, :] = dy[0:MAIN].astype(BF16)
    last = jnp.concatenate([x[MAIN:CAP], dy[MAIN:CAP]], axis=0)
    block[2 * MAIN : BLOCK, :] = last.astype(BF16)


def tails(blocks, turned):
    parts = []
    for block in blocks:
        last = block[2 * MAIN : BLOCK, :].astype(F32)
        if turned:
            last = jnp.concatenate([last[TAIL:], last[:TAIL]], axis=0)
        parts.append(last)
    return jnp.concatenate(parts, axis=0).astype(BF16)


def rows_of(blocks, first, turned):
    return jnp.concatenate(
        [block[first : first + MAIN, :] for block in blocks] + [tails(blocks, turned)], axis=0
    )


def front_kernel(mine, other, w_gate, w_up, w_down, part, sent):
    width = w_gate.shape[1]
    x = rows_of((mine, other), 0, False)
    dy = rows_of((mine, other), MAIN, True)
    for at, value in enumerate(
        (mul(x, w_gate[...]), mul(x, w_up[...]), mul(dy, w_down[...], 1, 1))
    ):
        part[:, at * width : (at + 1) * width] = value
        sent[:, at * width : (at + 1) * width] = value.astype(BF16)


def back_kernel(part, arrived, w_gate, w_up, hidden, d_pre, term, sent):
    width = w_gate.shape[1]
    sums = part[...] + arrived[...].astype(F32)
    z_gate, z_up, d_hidden = (sums[:, i * width : (i + 1) * width] for i in range(3))
    sig = jax.nn.sigmoid(z_gate)
    act = z_gate * sig
    row = lax.broadcasted_iota(jnp.int32, (GROUP, width), 0)
    real = (row < 2 * MAIN) | (row % 8 < TAIL)
    hidden[...] = jnp.where(real, act * z_up, 0.0).astype(BF16)
    d_gate = d_hidden * z_up * sig * (1.0 + z_gate * (1.0 - sig))
    d_gate = jnp.where(real, d_gate, 0.0).astype(BF16)
    d_up = jnp.where(real, d_hidden * act, 0.0).astype(BF16)
    d_pre[:, :width] = d_gate
    d_pre[:, width:] = d_up
    value = mul(d_gate, w_gate[...], 1, 1) + mul(d_up, w_up[...], 1, 1)
    term[0:MAIN, :] = value[0:MAIN]
    term[MAIN:TERM, :] = value[2 * MAIN : 2 * MAIN + 8]
    sent[0:MAIN, :] = value[MAIN : 2 * MAIN].astype(BF16)
    sent[MAIN:TERM, :] = value[2 * MAIN + 8 : GROUP].astype(BF16)


def add_kernel(term, arrived, total):
    total[...] = (term[...] + arrived[...].astype(F32)).astype(BF16)


def finish_kernel(placing_t, first, second, third, fourth, grad_in):
    total = first[...].astype(F32) + second[...].astype(F32)
    total = total + third[...].astype(F32) + fourth[...].astype(F32)
    grad_in[...] = mul(placing_t[:, :TERM], total.astype(BF16)).astype(BF16)


def grads_kernel(*refs):
    blocks, hiddens, d_pres = refs[0:8], refs[8:12], refs[12:16]
    grad_gate, grad_up, grad_down = refs[16:19]
    width = grad_gate.shape[1]

    def groups(values):
        return jnp.concatenate(
            [v[: 2 * MAIN, :] for v in values] + [v[2 * MAIN :, :] for v in values], axis=0
        )

    def rows(first, turned):
        return jnp.concatenate(
            [v[first : first + MAIN, :] for v in blocks]
            + [tails(blocks[i : i + 2], turned) for i in range(0, 8, 2)],
            axis=0,
        )

    d_pre, hidden = groups(d_pres), groups(hiddens)
    x = rows(0, False)
    grad_gate[...] = mul(x, d_pre[:, :width], 0, 0).astype(BF16)
    grad_up[...] = mul(x, d_pre[:, width:], 0, 0).astype(BF16)
    grad_down[...] = mul(hidden, rows(MAIN, True), 0, 0).astype(BF16)


def four_by_two(tokens, grad_out, expert_ids, gate_probs, w_gate, w_up, w_down):
    features, width = w_gate.shape

    def across(value):
        return lax.ppermute(value, "expert", [(i, i ^ 1) for i in range(8)])

    def along(value, distance):
        return lax.ppermute(value, "expert", [(i, i ^ (2 * distance)) for i in range(8)])

    def after(value, *others):
        return lax.optimization_barrier((value,) + others)[0]

    gate, up, down = (pltpu.with_memory_space_constraint(w, pltpu.VMEM) for w in (w_gate, w_up, w_down))

    own, placing_t = call(
        place_kernel,
        (struct(BLOCK, features, BF16), struct(tokens.shape[0], tokens.shape[0], BF16)),
        tokens, grad_out, expert_ids, gate_probs, name="place",
    )

    def front(mine, other):
        part, sent = call(
            front_kernel,
            (struct(GROUP, 3 * width, F32), struct(GROUP, 3 * width, BF16)),
            mine, other, gate, up, down, name="front",
        )
        return part, lax.ppermute(sent, "tensor", [(0, 1), (1, 0)])

    def back(part, arrived):
        hidden, d_pre, term, sent = call(
            back_kernel,
            (
                struct(GROUP, width, BF16),
                struct(GROUP, 2 * width, BF16),
                struct(TERM, features, F32),
                struct(TERM, features, BF16),
            ),
            part, arrived, gate, up, name="back",
        )
        total = call(add_kernel, struct(TERM, features, BF16), term, across(sent), name="add")
        return hidden, d_pre, total

    two = along(own, 2)
    one = along(own, 1)
    own_y = across(own)
    three = along(after(own, one), 3)
    one_y, two_y, three_y = across(one), across(two), across(three)

    h0, d0, q0 = back(*front(after(own, one), own_y))
    h1, d1, q1 = back(*front(after(one, two), one_y))
    r1 = along(q1, 1)
    h2, d2, q2 = back(*front(after(two, q0), two_y))
    r2 = along(q2, 2)
    h3, d3, q3 = back(*front(after(three, q2, r1), three_y))
    r3 = along(q3, 3)

    tile = features // 4
    column = pl.BlockSpec((BLOCK, tile), lambda j: (0, j))
    whole = [pl.BlockSpec((GROUP, width), lambda j: (0, 0))] * 4
    whole += [pl.BlockSpec((GROUP, 2 * width), lambda j: (0, 0))] * 4
    grads = call(
        grads_kernel,
        (struct(features, width, BF16), struct(features, width, BF16), struct(width, features, BF16)),
        after(own, q3), own_y, one, one_y, two, two_y, three, three_y, h0, h1, h2, h3, d0, d1, d2, d3,
        name="grads",
        grid=(features // tile,),
        in_specs=[column] * 8 + whole,
        out_specs=(
            pl.BlockSpec((tile, width), lambda j: (j, 0)),
            pl.BlockSpec((tile, width), lambda j: (j, 0)),
            pl.BlockSpec((width, tile), lambda j: (0, j)),
        ),
    )
    grads, r3 = lax.optimization_barrier((grads, r3))
    grad_in = call(
        finish_kernel, struct(tokens.shape[0], features, BF16), placing_t, q0, r1, r2, r3, name="finish"
    )
    return (grad_in,) + tuple(grads)


def solution(mesh):
    in_specs = (
        P(("pipe", "expert"), "tensor"),
        P(("pipe", "expert"), "tensor"),
        P(("pipe", "expert"), None),
        P(("pipe", "expert"), None),
        P("tensor", "expert"),
        P("tensor", "expert"),
        P("expert", "tensor"),
    )
    out_specs = (
        P(("pipe", "expert"), "tensor"),
        P(("pipe", "tensor"), "expert"),
        P(("pipe", "tensor"), "expert"),
        P(("pipe", "expert"), "tensor"),
    )
    small = mesh.shape["expert"] == 8 and mesh.shape["tensor"] == 2
    body = four_by_two if small else any_size
    return jax.shard_map(body, mesh=mesh, in_specs=in_specs, out_specs=out_specs, check_vma=False)
```

```python
import jax
import jax.numpy as jnp
from jax import lax
from jax.experimental import pallas as pl
from jax.experimental.pallas import tpu as pltpu
from jax.sharding import PartitionSpec as P

CAP = 36


window_expert = 0


def swiglu_grads(sums, width):
    z_gate = sums[:, :width]
    z_up = sums[:, width : 2 * width]
    d_hidden = sums[:, 2 * width :]
    sig = jax.nn.sigmoid(z_gate)
    act = z_gate * sig
    hidden = (act * z_up).astype(jnp.bfloat16)
    d_gate = (d_hidden * z_up * sig * (1.0 + z_gate * (1.0 - sig))).astype(jnp.bfloat16)
    d_up = (d_hidden * act).astype(jnp.bfloat16)
    return (hidden, jnp.concatenate([d_gate, d_up], axis=1))


def place(tokens, grad_out, expert_ids, gate_probs):
    chosen = expert_ids == window_expert
    weight = jnp.sum(jnp.where(chosen, gate_probs, jnp.zeros_like(gate_probs)), axis=1)
    scaled = (weight[:, None] * grad_out.astype(jnp.float32)).astype(jnp.bfloat16)
    routed = jnp.any(chosen, axis=1)
    slot_of = jnp.cumsum(routed.astype(jnp.int32)) - 1
    slot_ids = jnp.arange(CAP, dtype=jnp.int32)
    placing = ((slot_of[None, :] == slot_ids[:, None]) & routed[None, :]).astype(jnp.bfloat16)
    send_x = jnp.dot(placing, tokens, preferred_element_type=jnp.float32).astype(jnp.bfloat16)
    send_dy = jnp.dot(placing, scaled, preferred_element_type=jnp.float32).astype(jnp.bfloat16)
    return placing, send_x, send_dy


def unplace(placing, summed):
    return lax.dot_general(
        placing, summed, (((0,), (0,)), ((), ())), preferred_element_type=jnp.float32
    ).astype(jnp.bfloat16)


def weight_grads(rows_x, rows_dy, hidden, d_pre, width):
    grad_w_in = lax.dot_general(
        rows_x, d_pre, (((0,), (0,)), ((), ())), preferred_element_type=jnp.float32
    ).astype(jnp.bfloat16)
    grad_down = lax.dot_general(
        hidden, rows_dy, (((0,), (0,)), ((), ())), preferred_element_type=jnp.float32
    ).astype(jnp.bfloat16)
    return (grad_w_in[:, :width], grad_w_in[:, width:], grad_down)


def any_size(tokens, grad_out, expert_ids, gate_probs, w_gate, w_up, w_down):
    width = w_gate.shape[1]
    placing, send_x, send_dy = place(tokens, grad_out, expert_ids, gate_probs)
    rows_x, rows_dy = (
        lax.all_gather(send_x, "expert", axis=0, tiled=True),
        lax.all_gather(send_dy, "expert", axis=0, tiled=True),
    )
    w_in = jnp.concatenate([w_gate, w_up], axis=1)
    front = jnp.dot(rows_x, w_in, preferred_element_type=jnp.float32)
    back = lax.dot_general(
        rows_dy, w_down, (((1,), (1,)), ((), ())), preferred_element_type=jnp.float32
    )
    partial_value = jnp.concatenate([front, back], axis=1)
    share = lax.psum_scatter(
        partial_value.astype(jnp.bfloat16), "tensor", scatter_dimension=0, tiled=True
    ).astype(jnp.float32)
    hidden_part, grads_part = swiglu_grads(share, width)
    hidden, d_pre = (
        lax.all_gather(hidden_part, "tensor", axis=0, tiled=True),
        lax.all_gather(grads_part, "tensor", axis=0, tiled=True),
    )
    summed = lax.psum_scatter(
        lax.dot_general(
            d_pre, w_in, (((1,), (1,)), ((), ())), preferred_element_type=jnp.float32
        ).astype(jnp.bfloat16),
        "expert",
        scatter_dimension=0,
        tiled=True,
    )
    grad_in = unplace(placing, summed)
    return (grad_in,) + weight_grads(rows_x, rows_dy, hidden, d_pre, width)


MAIN = 32
TAIL = CAP - MAIN
BLOCK = 2 * CAP
TERM = 40
GROUP = 80
BF16, F32 = jnp.bfloat16, jnp.float32


def struct(rows, columns, dtype):
    return jax.ShapeDtypeStruct((rows, columns), dtype)


def call(kernel, outs, *args, name, **more):
    return pl.pallas_call(
        kernel,
        out_shape=outs,
        name=name,
        compiler_params=pltpu.CompilerParams(vmem_limit_bytes=24 * 2**20),
        cost_estimate=pl.CostEstimate(flops=1000, bytes_accessed=1000, transcendentals=0),
        **more,
    )(*args)


def mul(left, right, left_dim=1, right_dim=0):
    return lax.dot_general(
        left, right, (((left_dim,), (right_dim,)), ((), ())), preferred_element_type=F32
    )


def place_kernel(
    tokens_at, grad_out_at, ids_at, probs_at, block, placing_t, tokens, grad_out, ids, probs, done
):
    pairs = ((ids_at, ids), (probs_at, probs), (tokens_at, tokens), (grad_out_at, grad_out))
    copies = [pltpu.make_async_copy(a, b, done.at[i]) for i, (a, b) in enumerate(pairs)]
    for copy in copies:
        copy.start()
    rows = tokens.shape[0]
    copies[0].wait()
    copies[1].wait()
    chosen = ids[...] == window_expert
    weight_row = jnp.sum(jnp.where(chosen, probs[...], 0.0), axis=0, keepdims=True)
    routed_row = jnp.max(chosen.astype(F32), axis=0, keepdims=True)
    at_row = lax.broadcasted_iota(jnp.int32, (rows, rows), 0)
    at_column = lax.broadcasted_iota(jnp.int32, (rows, rows), 1)
    same = at_row == at_column
    routed = jnp.sum(jnp.where(same, routed_row, 0.0), axis=1, keepdims=True)
    slot_row = jnp.sum(jnp.where(at_row <= at_column, routed, 0.0), axis=0, keepdims=True) - 1.0
    slot = jnp.sum(jnp.where(at_column <= at_row, routed_row, 0.0), axis=1, keepdims=True) - 1.0
    wanted = lax.broadcasted_iota(jnp.int32, (TERM, rows), 0).astype(F32)
    placing = jnp.where((slot_row == wanted) & (routed_row > 0.0), 1.0, 0.0)
    wanted = at_column.astype(F32)
    placing_t[...] = jnp.where((slot == wanted) & (routed > 0.0), 1.0, 0.0).astype(BF16)
    scale = jnp.sum(placing * weight_row, axis=1, keepdims=True)
    placing = placing.astype(BF16)
    copies[2].wait()
    x = mul(placing, tokens[...])
    copies[3].wait()
    dy = mul(placing, grad_out[...]) * scale
    block[0:MAIN, :] = x[0:MAIN].astype(BF16)
    block[MAIN : 2 * MAIN, :] = dy[0:MAIN].astype(BF16)
    last = jnp.concatenate([x[MAIN:CAP], dy[MAIN:CAP]], axis=0)
    block[2 * MAIN : BLOCK, :] = last.astype(BF16)


def tails(blocks, turned):
    parts = []
    for block in blocks:
        last = block[2 * MAIN : BLOCK, :].astype(F32)
        if turned:
            last = jnp.concatenate([last[TAIL:], last[:TAIL]], axis=0)
        parts.append(last)
    return jnp.concatenate(parts, axis=0).astype(BF16)


def rows_of(blocks, first, turned):
    return jnp.concatenate(
        [block[first : first + MAIN, :] for block in blocks] + [tails(blocks, turned)], axis=0
    )


def front_kernel(mine, other, w_gate, w_up, w_down, part, sent):
    width = w_gate.shape[1]
    x = rows_of((mine, other), 0, False)
    dy = rows_of((mine, other), MAIN, True)
    for at, value in enumerate(
        (mul(x, w_gate[...]), mul(x, w_up[...]), mul(dy, w_down[...], 1, 1))
    ):
        part[:, at * width : (at + 1) * width] = value
        sent[:, at * width : (at + 1) * width] = value.astype(BF16)


def folded(main, last):
    half = main.shape[1] // 2
    return jnp.concatenate([main[:, :half], last[:, :half], main[:, half:], last[:, half:]], axis=0)


def back_kernel(part, arrived, w_gate, w_up, hidden, d_pre, term, sent):
    width = w_gate.shape[1]
    sums = part[...] + arrived[...].astype(F32)
    z_gate, z_up, d_hidden = (sums[:, i * width : (i + 1) * width] for i in range(3))
    sig = jax.nn.sigmoid(z_gate)
    act = z_gate * sig
    row = lax.broadcasted_iota(jnp.int32, (GROUP, width), 0)
    real = (row < 2 * MAIN) | (row % 8 < TAIL)
    hidden[...] = jnp.where(real, act * z_up, 0.0).astype(BF16)
    d_gate = d_hidden * z_up * sig * (1.0 + z_gate * (1.0 - sig))
    d_gate = jnp.where(real, d_gate, 0.0).astype(BF16)
    d_up = jnp.where(real, d_hidden * act, 0.0).astype(BF16)
    d_pre[:, :width] = d_gate
    d_pre[:, width:] = d_up
    value = mul(d_gate, w_gate[...], 1, 1) + mul(d_up, w_up[...], 1, 1)
    term[...] = folded(value[0:MAIN], value[2 * MAIN : 2 * MAIN + TAIL])
    sent[...] = folded(value[MAIN : 2 * MAIN], value[2 * MAIN + 8 : 2 * MAIN + 8 + TAIL]).astype(BF16)


def add_kernel(term, arrived, total):
    total[...] = (term[...] + arrived[...].astype(F32)).astype(BF16)


def finish_kernel(placing_t, first, second, third, fourth, grad_in):
    total = first[...].astype(F32) + second[...].astype(F32)
    total = total + third[...].astype(F32) + fourth[...].astype(F32)
    half = total.shape[1]
    placing = placing_t[:, :CAP]
    grad_in[:, :half] = mul(placing, total[:CAP].astype(BF16)).astype(BF16)
    grad_in[:, half:] = mul(placing, total[CAP:].astype(BF16)).astype(BF16)


def grads_kernel(*refs):
    blocks, hiddens, d_pres = refs[0:8], refs[8:12], refs[12:16]
    grad_gate, grad_up, grad_down = refs[16:19]
    width = grad_gate.shape[1]

    def groups(values):
        return jnp.concatenate(
            [v[: 2 * MAIN, :] for v in values] + [v[2 * MAIN :, :] for v in values], axis=0
        )

    def rows(first, turned):
        return jnp.concatenate(
            [v[first : first + MAIN, :] for v in blocks]
            + [tails(blocks[i : i + 2], turned) for i in range(0, 8, 2)],
            axis=0,
        )

    d_pre, hidden = groups(d_pres), groups(hiddens)
    x = rows(0, False)
    grad_gate[...] = mul(x, d_pre[:, :width], 0, 0).astype(BF16)
    grad_up[...] = mul(x, d_pre[:, width:], 0, 0).astype(BF16)
    grad_down[...] = mul(hidden, rows(MAIN, True), 0, 0).astype(BF16)


def four_by_two(tokens, grad_out, expert_ids, gate_probs, w_gate, w_up, w_down):
    features, width = w_gate.shape

    def across(value):
        return lax.ppermute(value, "expert", [(i, i ^ 1) for i in range(8)])

    def along(value, distance):
        return lax.ppermute(value, "expert", [(i, i ^ (2 * distance)) for i in range(8)])

    def after(value, *others):
        return lax.optimization_barrier((value,) + others)[0]

    gate, up, down = (pltpu.with_memory_space_constraint(w, pltpu.VMEM) for w in (w_gate, w_up, w_down))

    own, placing_t = call(
        place_kernel,
        (struct(BLOCK, features, BF16), struct(tokens.shape[0], tokens.shape[0], BF16)),
        tokens, grad_out, expert_ids.T, gate_probs.T, name="place",
        in_specs=[pl.BlockSpec(memory_space=pltpu.HBM)] * 4,
        scratch_shapes=[
            pltpu.VMEM(tokens.shape, BF16),
            pltpu.VMEM(tokens.shape, BF16),
            pltpu.VMEM(expert_ids.shape[::-1], jnp.int32),
            pltpu.VMEM(gate_probs.shape[::-1], F32),
            pltpu.SemaphoreType.DMA((4,)),
        ],
    )

    def front(mine, other):
        part, sent = call(
            front_kernel,
            (struct(GROUP, 3 * width, F32), struct(GROUP, 3 * width, BF16)),
            mine, other, gate, up, down, name="front",
        )
        return part, lax.ppermute(sent, "tensor", [(0, 1), (1, 0)])

    def back(part, arrived):
        hidden, d_pre, term, sent = call(
            back_kernel,
            (
                struct(GROUP, width, BF16),
                struct(GROUP, 2 * width, BF16),
                struct(BLOCK, features // 2, F32),
                struct(BLOCK, features // 2, BF16),
            ),
            part, arrived, gate, up, name="back",
        )
        return hidden, d_pre, term, sent

    def add(term, sent):
        return call(add_kernel, struct(BLOCK, features // 2, BF16), term, across(sent), name="add")

    own_y = across(own)
    two = along(own, 2)
    one = along(own, 1)
    h0, d0, t0, s0 = back(*front(own, own_y))
    two, one, s0 = lax.optimization_barrier((two, one, s0))
    middle = lax.ppermute(after(own, two), "expert", [(2, 4), (3, 5), (4, 2), (5, 3)])
    ends = lax.ppermute(two, "expert", [(4, 6), (5, 7), (2, 0), (3, 1)])
    two_y = across(two)
    q0 = add(t0, s0)
    three = after(middle + ends, q0)
    three_y = across(three)
    one_y = along(after(own_y, three), 1)
    h2, d2, t2, s2 = back(*front(after(two, three), two_y))
    q2 = add(t2, s2)
    r2 = along(q2, 2)
    h1, d1, t1, s1 = back(*front(one, one_y))
    q1 = add(t1, s1)
    r1 = along(q1, 1)
    h3, d3, t3, s3 = back(*front(after(three, q2, s1), three_y))
    q3 = add(after(t3, r2), s3)
    r3 = along(q3, 3)

    tile = features // 4
    column = pl.BlockSpec((BLOCK, tile), lambda j: (0, j))
    whole = [pl.BlockSpec((GROUP, width), lambda j: (0, 0))] * 4
    whole += [pl.BlockSpec((GROUP, 2 * width), lambda j: (0, 0))] * 4
    grads = call(
        grads_kernel,
        (struct(features, width, BF16), struct(features, width, BF16), struct(width, features, BF16)),
        after(own, q3, r1), own_y, one, one_y, two, two_y, three, three_y, h0, h1, h2, h3, d0, d1, d2, d3,
        name="grads",
        grid=(features // tile,),
        in_specs=[column] * 8 + whole,
        out_specs=(
            pl.BlockSpec((tile, width), lambda j: (j, 0)),
            pl.BlockSpec((tile, width), lambda j: (j, 0)),
            pl.BlockSpec((width, tile), lambda j: (0, j)),
        ),
    )
    grads, r3 = lax.optimization_barrier((grads, r3))
    grad_in = call(
        finish_kernel, struct(tokens.shape[0], features, BF16), placing_t, q0, r1, r2, r3, name="finish"
    )
    return (grad_in,) + tuple(grads)


def solution(mesh):
    in_specs = (
        P(("pipe", "expert"), "tensor"),
        P(("pipe", "expert"), "tensor"),
        P(("pipe", "expert"), None),
        P(("pipe", "expert"), None),
        P("tensor", "expert"),
        P("tensor", "expert"),
        P("expert", "tensor"),
    )
    out_specs = (
        P(("pipe", "expert"), "tensor"),
        P(("pipe", "tensor"), "expert"),
        P(("pipe", "tensor"), "expert"),
        P(("pipe", "expert"), "tensor"),
    )
    small = mesh.shape["expert"] == 8 and mesh.shape["tensor"] == 2
    body = four_by_two if small else any_size
    return jax.shard_map(body, mesh=mesh, in_specs=in_specs, out_specs=out_specs, check_vma=False)
```

```python
import jax
import jax.numpy as jnp
from jax import lax
from jax.experimental import pallas as pl
from jax.experimental.pallas import tpu as pltpu
from jax.sharding import PartitionSpec as P

CAP = 36


window_expert = 0


def swiglu_grads(sums, width):
    z_gate = sums[:, :width]
    z_up = sums[:, width : 2 * width]
    d_hidden = sums[:, 2 * width :]
    sig = jax.nn.sigmoid(z_gate)
    act = z_gate * sig
    hidden = (act * z_up).astype(jnp.bfloat16)
    d_gate = (d_hidden * z_up * sig * (1.0 + z_gate * (1.0 - sig))).astype(jnp.bfloat16)
    d_up = (d_hidden * act).astype(jnp.bfloat16)
    return (hidden, jnp.concatenate([d_gate, d_up], axis=1))


def place(tokens, grad_out, expert_ids, gate_probs):
    chosen = expert_ids == window_expert
    weight = jnp.sum(jnp.where(chosen, gate_probs, jnp.zeros_like(gate_probs)), axis=1)
    scaled = (weight[:, None] * grad_out.astype(jnp.float32)).astype(jnp.bfloat16)
    routed = jnp.any(chosen, axis=1)
    slot_of = jnp.cumsum(routed.astype(jnp.int32)) - 1
    slot_ids = jnp.arange(CAP, dtype=jnp.int32)
    placing = ((slot_of[None, :] == slot_ids[:, None]) & routed[None, :]).astype(jnp.bfloat16)
    send_x = jnp.dot(placing, tokens, preferred_element_type=jnp.float32).astype(jnp.bfloat16)
    send_dy = jnp.dot(placing, scaled, preferred_element_type=jnp.float32).astype(jnp.bfloat16)
    return placing, send_x, send_dy


def unplace(placing, summed):
    return lax.dot_general(
        placing, summed, (((0,), (0,)), ((), ())), preferred_element_type=jnp.float32
    ).astype(jnp.bfloat16)


def weight_grads(rows_x, rows_dy, hidden, d_pre, width):
    grad_w_in = lax.dot_general(
        rows_x, d_pre, (((0,), (0,)), ((), ())), preferred_element_type=jnp.float32
    ).astype(jnp.bfloat16)
    grad_down = lax.dot_general(
        hidden, rows_dy, (((0,), (0,)), ((), ())), preferred_element_type=jnp.float32
    ).astype(jnp.bfloat16)
    return (grad_w_in[:, :width], grad_w_in[:, width:], grad_down)


def any_size(tokens, grad_out, expert_ids, gate_probs, w_gate, w_up, w_down):
    width = w_gate.shape[1]
    placing, send_x, send_dy = place(tokens, grad_out, expert_ids, gate_probs)
    rows_x, rows_dy = (
        lax.all_gather(send_x, "expert", axis=0, tiled=True),
        lax.all_gather(send_dy, "expert", axis=0, tiled=True),
    )
    w_in = jnp.concatenate([w_gate, w_up], axis=1)
    front = jnp.dot(rows_x, w_in, preferred_element_type=jnp.float32)
    back = lax.dot_general(
        rows_dy, w_down, (((1,), (1,)), ((), ())), preferred_element_type=jnp.float32
    )
    partial_value = jnp.concatenate([front, back], axis=1)
    share = lax.psum_scatter(
        partial_value.astype(jnp.bfloat16), "tensor", scatter_dimension=0, tiled=True
    ).astype(jnp.float32)
    hidden_part, grads_part = swiglu_grads(share, width)
    hidden, d_pre = (
        lax.all_gather(hidden_part, "tensor", axis=0, tiled=True),
        lax.all_gather(grads_part, "tensor", axis=0, tiled=True),
    )
    summed = lax.psum_scatter(
        lax.dot_general(
            d_pre, w_in, (((1,), (1,)), ((), ())), preferred_element_type=jnp.float32
        ).astype(jnp.bfloat16),
        "expert",
        scatter_dimension=0,
        tiled=True,
    )
    grad_in = unplace(placing, summed)
    return (grad_in,) + weight_grads(rows_x, rows_dy, hidden, d_pre, width)


MAIN = 32
TAIL = CAP - MAIN
BLOCK = 2 * CAP
TERM = 40
GROUP = 80
BF16, F32 = jnp.bfloat16, jnp.float32


def struct(rows, columns, dtype):
    return jax.ShapeDtypeStruct((rows, columns), dtype)


def call(kernel, outs, *args, name, **more):
    return pl.pallas_call(
        kernel,
        out_shape=outs,
        name=name,
        compiler_params=pltpu.CompilerParams(vmem_limit_bytes=24 * 2**20),
        cost_estimate=pl.CostEstimate(flops=1000, bytes_accessed=1000, transcendentals=0),
        **more,
    )(*args)


def mul(left, right, left_dim=1, right_dim=0):
    return lax.dot_general(
        left, right, (((left_dim,), (right_dim,)), ((), ())), preferred_element_type=F32
    )


def place_kernel(
    tokens_at, grad_out_at, ids_at, probs_at, block, placing_t, tokens, grad_out, ids, probs, done
):
    pairs = ((ids_at, ids), (probs_at, probs), (tokens_at, tokens), (grad_out_at, grad_out))
    copies = [pltpu.make_async_copy(a, b, done.at[i]) for i, (a, b) in enumerate(pairs)]
    for copy in copies:
        copy.start()
    rows = tokens.shape[0]
    copies[0].wait()
    copies[1].wait()
    chosen = ids[...] == window_expert
    weight_row = jnp.sum(jnp.where(chosen, probs[...], 0.0), axis=0, keepdims=True)
    routed_row = jnp.max(chosen.astype(F32), axis=0, keepdims=True)
    at_row = lax.broadcasted_iota(jnp.int32, (rows, rows), 0)
    at_column = lax.broadcasted_iota(jnp.int32, (rows, rows), 1)
    same = at_row == at_column
    routed = jnp.sum(jnp.where(same, routed_row, 0.0), axis=1, keepdims=True)
    slot_row = jnp.sum(jnp.where(at_row <= at_column, routed, 0.0), axis=0, keepdims=True) - 1.0
    slot = jnp.sum(jnp.where(at_column <= at_row, routed_row, 0.0), axis=1, keepdims=True) - 1.0
    wanted = lax.broadcasted_iota(jnp.int32, (TERM, rows), 0).astype(F32)
    placing = jnp.where((slot_row == wanted) & (routed_row > 0.0), 1.0, 0.0)
    wanted = at_column.astype(F32)
    placing_t[...] = jnp.where((slot == wanted) & (routed > 0.0), 1.0, 0.0).astype(BF16)
    scale = jnp.sum(placing * weight_row, axis=1, keepdims=True)
    placing = placing.astype(BF16)
    copies[2].wait()
    x = mul(placing, tokens[...])
    copies[3].wait()
    dy = mul(placing, grad_out[...]) * scale
    last = jnp.concatenate([x[MAIN:CAP], dy[MAIN:CAP]], axis=0)
    for at, value in ((0, x[0:MAIN]), (MAIN, dy[0:MAIN]), (2 * MAIN, last)):
        block[at : at + value.shape[0], :] = value.astype(BF16)


def tails(blocks, turned, columns):
    parts = []
    for block in blocks:
        last = block[2 * MAIN : BLOCK, columns].astype(F32)
        if turned:
            last = jnp.concatenate([last[TAIL:], last[:TAIL]], axis=0)
        parts.append(last)
    return jnp.concatenate(parts, axis=0).astype(BF16)


def rows_of(blocks, first, turned, columns):
    main = [block[first : first + MAIN, columns] for block in blocks]
    last = [tails(blocks[i : i + 2], turned, columns) for i in range(0, len(blocks), 2)]
    return jnp.concatenate(main + last, axis=0)


def front_kernel(mine, other, w_gate, w_up, w_down, part, sent):
    width = w_gate.shape[1]
    x = rows_of((mine, other), 0, False, slice(None))
    dy = rows_of((mine, other), MAIN, True, slice(None))
    for at, value in enumerate((mul(x, w_gate[...]), mul(x, w_up[...]), mul(dy, w_down[...], 1, 1))):
        part[:, at * width : (at + 1) * width] = value
        sent[:, at * width : (at + 1) * width] = value.astype(BF16)


def folded(main, last):
    half = main.shape[1] // 2
    return jnp.concatenate([main[:, :half], last[:, :half], main[:, half:], last[:, half:]], axis=0)


def back_kernel(part, arrived, w_gate, w_up, hidden, d_pre, term, sent):
    width = w_gate.shape[1]
    sums = part[...] + arrived[...].astype(F32)
    z_gate, z_up, d_hidden = (sums[:, i * width : (i + 1) * width] for i in range(3))
    sig = jax.nn.sigmoid(z_gate)
    act = z_gate * sig
    row = lax.broadcasted_iota(jnp.int32, (GROUP, width), 0)
    real = (row < 2 * MAIN) | (row % 8 < TAIL)
    hidden[...] = jnp.where(real, act * z_up, 0.0).astype(BF16)
    d_gate = d_hidden * z_up * sig * (1.0 + z_gate * (1.0 - sig))
    d_gate = jnp.where(real, d_gate, 0.0).astype(BF16)
    d_up = jnp.where(real, d_hidden * act, 0.0).astype(BF16)
    d_pre[:, :width] = d_gate
    d_pre[:, width:] = d_up
    value = mul(d_gate, w_gate[...], 1, 1) + mul(d_up, w_up[...], 1, 1)
    term[...] = folded(value[0:MAIN], value[2 * MAIN : 2 * MAIN + TAIL])
    sent[...] = folded(value[MAIN : 2 * MAIN], value[2 * MAIN + 8 : 2 * MAIN + 8 + TAIL]).astype(BF16)


def add_kernel(term, arrived, total):
    total[...] = (term[...] + arrived[...].astype(F32)).astype(BF16)


def near_kernel(first, second, third, total):
    total[...] = first[...].astype(F32) + second[...].astype(F32) + third[...].astype(F32)


def finish_kernel(placing_t, near, last, grad_in):
    total = near[...] + last[...].astype(F32)
    half = total.shape[1]
    placing = placing_t[:, :CAP]
    grad_in[:, :half] = mul(placing, total[:CAP].astype(BF16)).astype(BF16)
    grad_in[:, half:] = mul(placing, total[CAP:].astype(BF16)).astype(BF16)


def grads_kernel(*refs):
    blocks, hiddens, d_pres, outs, tiles, done = refs[:8], refs[8:12], refs[12:16], refs[16:19], refs[19:22], refs[22]
    features, width = outs[0].shape
    size = features // 4

    def groups(values):
        return jnp.concatenate(
            [v[: 2 * MAIN, :] for v in values] + [v[2 * MAIN :, :] for v in values], axis=0
        )

    d_pre, hidden = groups(d_pres), groups(hiddens)
    copies = []
    for step in range(4):
        at = slice(step * size, (step + 1) * size)
        x = rows_of(blocks, 0, False, at)
        tiles[0][at, :] = mul(x, d_pre[:, :width], 0, 0).astype(BF16)
        tiles[1][at, :] = mul(x, d_pre[:, width:], 0, 0).astype(BF16)
        tiles[2][:, at] = mul(hidden, rows_of(blocks, MAIN, True, at), 0, 0).astype(BF16)
        for i, place in enumerate(((at, slice(None)), (at, slice(None)), (slice(None), at))):
            copy = pltpu.make_async_copy(tiles[i].at[place], outs[i].at[place], done.at[3 * step + i])
            copy.start()
            copies.append(copy)
    for copy in copies:
        copy.wait()


def load_kernel(*refs):
    copies = [pltpu.make_async_copy(refs[i], refs[3 + i], refs[6].at[i]) for i in range(3)]
    for copy in copies:
        copy.start()
    for copy in copies:
        copy.wait()


def four_by_two(tokens, grad_out, expert_ids, gate_probs, w_gate, w_up, w_down):
    features, width = w_gate.shape
    half = features // 2
    in_hbm = pl.BlockSpec(memory_space=pltpu.HBM)

    def across(value):
        return lax.ppermute(value, "expert", [(i, i ^ 1) for i in range(8)])

    def along(value, distance):
        return lax.ppermute(value, "expert", [(i, i ^ (2 * distance)) for i in range(8)])

    def after(value, *others):
        return lax.optimization_barrier((value,) + others)[0]

    def hbm(value):
        return pltpu.with_memory_space_constraint(value, pltpu.HBM)

    own, placing_t = call(
        place_kernel,
        (
            struct(BLOCK, features, BF16),
            struct(tokens.shape[0], tokens.shape[0], BF16),
        ),
        hbm(tokens), hbm(grad_out), hbm(expert_ids.T), hbm(gate_probs.T), name="place",
        in_specs=[in_hbm] * 4,
        scratch_shapes=[
            pltpu.VMEM(tokens.shape, BF16),
            pltpu.VMEM(tokens.shape, BF16),
            pltpu.VMEM(expert_ids.shape[::-1], jnp.int32),
            pltpu.VMEM(gate_probs.shape[::-1], F32),
            pltpu.SemaphoreType.DMA((4,)),
        ],
    )
    w_gate, w_up, w_down, _ = lax.optimization_barrier((w_gate, w_up, w_down, own))
    gate, up, down = call(
        load_kernel,
        tuple(struct(*w.shape, BF16) for w in (w_gate, w_up, w_down)),
        hbm(w_gate), hbm(w_up), hbm(w_down), name="load",
        in_specs=[in_hbm] * 3,
        scratch_shapes=[pltpu.SemaphoreType.DMA((3,))],
    )

    def front(mine, other):
        part, sent = call(
            front_kernel,
            (struct(GROUP, 3 * width, F32), struct(GROUP, 3 * width, BF16)),
            mine, other, gate, up, down, name="front",
        )
        return part, lax.ppermute(sent, "tensor", [(0, 1), (1, 0)])

    def back(part, arrived):
        return call(
            back_kernel,
            (
                struct(GROUP, width, BF16),
                struct(GROUP, 2 * width, BF16),
                struct(BLOCK, half, F32),
                struct(BLOCK, half, BF16),
            ),
            part, arrived, gate, up, name="back",
        )

    def add(term, sent):
        return call(add_kernel, struct(BLOCK, half, BF16), term, across(sent), name="add")

    def middle(value):
        return lax.ppermute(value, "expert", [(2, 4), (3, 5), (4, 2), (5, 3)])

    def ends(value):
        return lax.ppermute(value, "expert", [(4, 6), (5, 7), (2, 0), (3, 1)])

    own_y = across(own)
    two = along(own, 2)
    one = along(own, 1)
    h0, d0, t0, s0 = back(*front(own, own_y))
    one_y = along(own_y, 1)
    q0 = add(t0, s0)
    two, one, q0 = lax.optimization_barrier((two, one, q0))
    inner = middle(after(own, two))
    outer = ends(two)
    two_y = across(two)
    h1, d1, t1, s1 = back(*front(one, one_y))
    q1 = add(t1, s1)
    inner, two_y, s1 = lax.optimization_barrier((inner, two_y, s1))
    inner_y = middle(after(own_y, inner))
    outer_y = ends(two_y)
    three = inner + outer
    three_y = inner_y + outer_y
    part2, swap2 = front(two, two_y)
    h2, d2, t2, s2 = back(after(part2, three, q1), swap2)
    q2 = add(t2, s2)
    r2 = along(q2, 2)
    h3, d3, t3, s3 = back(*front(after(three, q2), three_y))
    r1 = along(after(q1, s3), 1)
    q3 = add(after(t3, r2), s3)
    r3 = along(q3, 3)

    grads = call(
        grads_kernel,
        (struct(features, width, BF16), struct(features, width, BF16), struct(width, features, BF16)),
        after(own, q3), own_y, one, one_y, two, two_y, three, three_y, h0, h1, h2, h3, d0, d1, d2, d3,
        name="grads",
        out_specs=(pl.BlockSpec(memory_space=pltpu.HBM),) * 3,
        scratch_shapes=[
            pltpu.VMEM(w_gate.shape, BF16),
            pltpu.VMEM(w_up.shape, BF16),
            pltpu.VMEM(w_down.shape, BF16),
            pltpu.SemaphoreType.DMA((12,)),
        ],
    )
    grads, r2, r1 = lax.optimization_barrier((grads, r2, r1))
    near = call(near_kernel, struct(BLOCK, half, F32), q0, r1, r2, name="near")
    grad_in = call(
        finish_kernel, struct(tokens.shape[0], features, BF16), placing_t, near, after(r3, near), name="finish"
    )
    return (grad_in,) + tuple(grads)


def solution(mesh):
    in_specs = (
        P(("pipe", "expert"), "tensor"),
        P(("pipe", "expert"), "tensor"),
        P(("pipe", "expert"), None),
        P(("pipe", "expert"), None),
        P("tensor", "expert"),
        P("tensor", "expert"),
        P("expert", "tensor"),
    )
    out_specs = (
        P(("pipe", "expert"), "tensor"),
        P(("pipe", "tensor"), "expert"),
        P(("pipe", "tensor"), "expert"),
        P(("pipe", "expert"), "tensor"),
    )
    small = mesh.shape["expert"] == 8 and mesh.shape["tensor"] == 2
    body = four_by_two if small else any_size
    return jax.shard_map(body, mesh=mesh, in_specs=in_specs, out_specs=out_specs, check_vma=False)
```

```python
import jax
import jax.numpy as jnp
from jax import lax
from jax.experimental import pallas as pl
from jax.experimental.pallas import tpu as pltpu
from jax.sharding import PartitionSpec as P

CAP = 36


window_expert = 0


def swiglu_grads(sums, width):
    z_gate = sums[:, :width]
    z_up = sums[:, width : 2 * width]
    d_hidden = sums[:, 2 * width :]
    sig = jax.nn.sigmoid(z_gate)
    act = z_gate * sig
    hidden = (act * z_up).astype(jnp.bfloat16)
    d_gate = (d_hidden * z_up * sig * (1.0 + z_gate * (1.0 - sig))).astype(jnp.bfloat16)
    d_up = (d_hidden * act).astype(jnp.bfloat16)
    return (hidden, jnp.concatenate([d_gate, d_up], axis=1))


def place(tokens, grad_out, expert_ids, gate_probs):
    chosen = expert_ids == window_expert
    weight = jnp.sum(jnp.where(chosen, gate_probs, jnp.zeros_like(gate_probs)), axis=1)
    scaled = (weight[:, None] * grad_out.astype(jnp.float32)).astype(jnp.bfloat16)
    routed = jnp.any(chosen, axis=1)
    slot_of = jnp.cumsum(routed.astype(jnp.int32)) - 1
    slot_ids = jnp.arange(CAP, dtype=jnp.int32)
    placing = ((slot_of[None, :] == slot_ids[:, None]) & routed[None, :]).astype(jnp.bfloat16)
    send_x = jnp.dot(placing, tokens, preferred_element_type=jnp.float32).astype(jnp.bfloat16)
    send_dy = jnp.dot(placing, scaled, preferred_element_type=jnp.float32).astype(jnp.bfloat16)
    return placing, send_x, send_dy


def unplace(placing, summed):
    return lax.dot_general(
        placing, summed, (((0,), (0,)), ((), ())), preferred_element_type=jnp.float32
    ).astype(jnp.bfloat16)


def weight_grads(rows_x, rows_dy, hidden, d_pre, width):
    grad_w_in = lax.dot_general(
        rows_x, d_pre, (((0,), (0,)), ((), ())), preferred_element_type=jnp.float32
    ).astype(jnp.bfloat16)
    grad_down = lax.dot_general(
        hidden, rows_dy, (((0,), (0,)), ((), ())), preferred_element_type=jnp.float32
    ).astype(jnp.bfloat16)
    return (grad_w_in[:, :width], grad_w_in[:, width:], grad_down)


def any_size(tokens, grad_out, expert_ids, gate_probs, w_gate, w_up, w_down):
    width = w_gate.shape[1]
    placing, send_x, send_dy = place(tokens, grad_out, expert_ids, gate_probs)
    rows_x, rows_dy = (
        lax.all_gather(send_x, "expert", axis=0, tiled=True),
        lax.all_gather(send_dy, "expert", axis=0, tiled=True),
    )
    w_in = jnp.concatenate([w_gate, w_up], axis=1)
    front = jnp.dot(rows_x, w_in, preferred_element_type=jnp.float32)
    back = lax.dot_general(
        rows_dy, w_down, (((1,), (1,)), ((), ())), preferred_element_type=jnp.float32
    )
    partial_value = jnp.concatenate([front, back], axis=1)
    share = lax.psum_scatter(
        partial_value.astype(jnp.bfloat16), "tensor", scatter_dimension=0, tiled=True
    ).astype(jnp.float32)
    hidden_part, grads_part = swiglu_grads(share, width)
    hidden, d_pre = (
        lax.all_gather(hidden_part, "tensor", axis=0, tiled=True),
        lax.all_gather(grads_part, "tensor", axis=0, tiled=True),
    )
    summed = lax.psum_scatter(
        lax.dot_general(
            d_pre, w_in, (((1,), (1,)), ((), ())), preferred_element_type=jnp.float32
        ).astype(jnp.bfloat16),
        "expert",
        scatter_dimension=0,
        tiled=True,
    )
    grad_in = unplace(placing, summed)
    return (grad_in,) + weight_grads(rows_x, rows_dy, hidden, d_pre, width)


MAIN = 32
TAIL = CAP - MAIN
BLOCK = 2 * CAP
TERM = 40
GROUP = 80
BF16, F32 = jnp.bfloat16, jnp.float32


def struct(rows, columns, dtype):
    return jax.ShapeDtypeStruct((rows, columns), dtype)


def call(kernel, outs, *args, name, **more):
    return pl.pallas_call(
        kernel,
        out_shape=outs,
        name=name,
        compiler_params=pltpu.CompilerParams(vmem_limit_bytes=24 * 2**20),
        cost_estimate=pl.CostEstimate(flops=1000, bytes_accessed=1000, transcendentals=0),
        **more,
    )(*args)


def mul(left, right, left_dim=1, right_dim=0):
    return lax.dot_general(
        left, right, (((left_dim,), (right_dim,)), ((), ())), preferred_element_type=F32
    )


def place_kernel(
    tokens_at, grad_out_at, ids_at, probs_at, block, placing_t, tokens, grad_out, ids, probs, done
):
    pairs = ((ids_at, ids), (probs_at, probs), (tokens_at, tokens), (grad_out_at, grad_out))
    copies = [pltpu.make_async_copy(a, b, done.at[i]) for i, (a, b) in enumerate(pairs)]
    for copy in copies:
        copy.start()
    rows = tokens.shape[0]
    copies[0].wait()
    copies[1].wait()
    chosen = ids[...] == window_expert
    weight_row = jnp.sum(jnp.where(chosen, probs[...], 0.0), axis=0, keepdims=True)
    routed_row = jnp.max(chosen.astype(F32), axis=0, keepdims=True)
    at_row = lax.broadcasted_iota(jnp.int32, (rows, rows), 0)
    at_column = lax.broadcasted_iota(jnp.int32, (rows, rows), 1)
    same = at_row == at_column
    routed = jnp.sum(jnp.where(same, routed_row, 0.0), axis=1, keepdims=True)
    slot_row = jnp.sum(jnp.where(at_row <= at_column, routed, 0.0), axis=0, keepdims=True) - 1.0
    slot = jnp.sum(jnp.where(at_column <= at_row, routed_row, 0.0), axis=1, keepdims=True) - 1.0
    wanted = lax.broadcasted_iota(jnp.int32, (TERM, rows), 0).astype(F32)
    placing = jnp.where((slot_row == wanted) & (routed_row > 0.0), 1.0, 0.0)
    wanted = at_column.astype(F32)
    placing_t[...] = jnp.where((slot == wanted) & (routed > 0.0), 1.0, 0.0).astype(BF16)
    scale = jnp.sum(placing * weight_row, axis=1, keepdims=True)
    placing = placing.astype(BF16)
    copies[2].wait()
    x = mul(placing, tokens[...])
    copies[3].wait()
    dy = mul(placing, grad_out[...]) * scale
    last = jnp.concatenate([x[MAIN:CAP], dy[MAIN:CAP]], axis=0)
    for at, value in ((0, x[0:MAIN]), (MAIN, dy[0:MAIN]), (2 * MAIN, last)):
        block[at : at + value.shape[0], :] = value.astype(BF16)


def tails(blocks, turned, columns):
    parts = []
    for block in blocks:
        last = block[2 * MAIN : BLOCK, columns].astype(F32)
        if turned:
            last = jnp.concatenate([last[TAIL:], last[:TAIL]], axis=0)
        parts.append(last)
    return jnp.concatenate(parts, axis=0).astype(BF16)


def rows_of(blocks, first, turned, columns):
    main = [block[first : first + MAIN, columns] for block in blocks]
    last = [tails(blocks[i : i + 2], turned, columns) for i in range(0, len(blocks), 2)]
    return jnp.concatenate(main + last, axis=0)


def front_kernel(mine, other, w_gate, w_up, w_down, part, sent):
    width = w_gate.shape[1]
    x = rows_of((mine, other), 0, False, slice(None))
    dy = rows_of((mine, other), MAIN, True, slice(None))
    for at, value in enumerate((mul(x, w_gate[...]), mul(x, w_up[...]), mul(dy, w_down[...], 1, 1))):
        part[:, at * width : (at + 1) * width] = value
        sent[:, at * width : (at + 1) * width] = value.astype(BF16)


def folded(main, last):
    half = main.shape[1] // 2
    return jnp.concatenate([main[:, :half], last[:, :half], main[:, half:], last[:, half:]], axis=0)


def back_kernel(part, arrived, w_gate, w_up, hidden, d_pre, term, sent):
    width = w_gate.shape[1]
    sums = part[...] + arrived[...].astype(F32)
    z_gate, z_up, d_hidden = (sums[:, i * width : (i + 1) * width] for i in range(3))
    sig = jax.nn.sigmoid(z_gate)
    act = z_gate * sig
    row = lax.broadcasted_iota(jnp.int32, (GROUP, width), 0)
    real = (row < 2 * MAIN) | (row % 8 < TAIL)
    hidden[...] = jnp.where(real, act * z_up, 0.0).astype(BF16)
    d_gate = d_hidden * z_up * sig * (1.0 + z_gate * (1.0 - sig))
    d_gate = jnp.where(real, d_gate, 0.0).astype(BF16)
    d_up = jnp.where(real, d_hidden * act, 0.0).astype(BF16)
    d_pre[:, :width] = d_gate
    d_pre[:, width:] = d_up
    value = mul(d_gate, w_gate[...], 1, 1) + mul(d_up, w_up[...], 1, 1)
    term[...] = folded(value[0:MAIN], value[2 * MAIN : 2 * MAIN + TAIL])
    sent[...] = folded(value[MAIN : 2 * MAIN], value[2 * MAIN + 8 : 2 * MAIN + 8 + TAIL]).astype(BF16)


def add_kernel(term, arrived, total):
    total[...] = (term[...] + arrived[...].astype(F32)).astype(BF16)


def is_inner():
    line = lax.axis_index("expert") // 2
    return (line == 1) | (line == 2)


def last_kernel(term, arrived, passed, total):
    value = term[...] + arrived[...].astype(F32)
    total[...] = jnp.where(is_inner(), value + passed[...].astype(F32), value).astype(BF16)


def near_kernel(first, second, passed, total):
    value = first[...].astype(F32) + second[...].astype(F32)
    total[...] = jnp.where(is_inner(), value, value + passed[...].astype(F32))


def finish_kernel(placing_t, near, last, grad_in):
    total = near[...] + last[...].astype(F32)
    half = total.shape[1]
    placing = placing_t[:, :CAP]
    grad_in[:, :half] = mul(placing, total[:CAP].astype(BF16)).astype(BF16)
    grad_in[:, half:] = mul(placing, total[CAP:].astype(BF16)).astype(BF16)


def grads_kernel(*refs):
    blocks, hiddens, d_pres, outs, tiles, done = refs[:8], refs[8:12], refs[12:16], refs[16:19], refs[19:22], refs[22]
    features, width = outs[0].shape
    size = features // 4

    def groups(values):
        return jnp.concatenate(
            [v[: 2 * MAIN, :] for v in values] + [v[2 * MAIN :, :] for v in values], axis=0
        )

    d_pre, hidden = groups(d_pres), groups(hiddens)
    copies = []
    for step in range(4):
        at = slice(step * size, (step + 1) * size)
        x = rows_of(blocks, 0, False, at)
        tiles[0][at, :] = mul(x, d_pre[:, :width], 0, 0).astype(BF16)
        tiles[1][at, :] = mul(x, d_pre[:, width:], 0, 0).astype(BF16)
        tiles[2][:, at] = mul(hidden, rows_of(blocks, MAIN, True, at), 0, 0).astype(BF16)
        for i, place in enumerate(((at, slice(None)), (at, slice(None)), (slice(None), at))):
            copy = pltpu.make_async_copy(tiles[i].at[place], outs[i].at[place], done.at[3 * step + i])
            copy.start()
            copies.append(copy)
    for copy in copies:
        copy.wait()


def load_kernel(*refs):
    copies = [pltpu.make_async_copy(refs[i], refs[3 + i], refs[6].at[i]) for i in range(3)]
    for copy in copies:
        copy.start()
    for copy in copies:
        copy.wait()


def four_by_two(tokens, grad_out, expert_ids, gate_probs, w_gate, w_up, w_down):
    features, width = w_gate.shape
    half = features // 2
    in_hbm = pl.BlockSpec(memory_space=pltpu.HBM)

    def across(value):
        return lax.ppermute(value, "expert", [(i, i ^ 1) for i in range(8)])

    def along(value, distance):
        return lax.ppermute(value, "expert", [(i, i ^ (2 * distance)) for i in range(8)])

    def after(value, *others):
        return lax.optimization_barrier((value,) + others)[0]

    def hbm(value):
        return pltpu.with_memory_space_constraint(value, pltpu.HBM)

    own, placing_t = call(
        place_kernel,
        (
            struct(BLOCK, features, BF16),
            struct(tokens.shape[0], tokens.shape[0], BF16),
        ),
        hbm(tokens), hbm(grad_out), hbm(expert_ids.T), hbm(gate_probs.T), name="place",
        in_specs=[in_hbm] * 4,
        scratch_shapes=[
            pltpu.VMEM(tokens.shape, BF16),
            pltpu.VMEM(tokens.shape, BF16),
            pltpu.VMEM(expert_ids.shape[::-1], jnp.int32),
            pltpu.VMEM(gate_probs.shape[::-1], F32),
            pltpu.SemaphoreType.DMA((4,)),
        ],
    )
    w_gate, w_up, w_down, _ = lax.optimization_barrier((w_gate, w_up, w_down, own))
    gate, up, down = call(
        load_kernel,
        tuple(struct(*w.shape, BF16) for w in (w_gate, w_up, w_down)),
        hbm(w_gate), hbm(w_up), hbm(w_down), name="load",
        in_specs=[in_hbm] * 3,
        scratch_shapes=[pltpu.SemaphoreType.DMA((3,))],
    )

    def front(mine, other):
        part, sent = call(
            front_kernel,
            (struct(GROUP, 3 * width, F32), struct(GROUP, 3 * width, BF16)),
            mine, other, gate, up, down, name="front",
        )
        return part, lax.ppermute(sent, "tensor", [(0, 1), (1, 0)])

    def back(part, arrived):
        return call(
            back_kernel,
            (
                struct(GROUP, width, BF16),
                struct(GROUP, 2 * width, BF16),
                struct(BLOCK, half, F32),
                struct(BLOCK, half, BF16),
            ),
            part, arrived, gate, up, name="back",
        )

    def add(term, sent):
        return call(add_kernel, struct(BLOCK, half, BF16), term, across(sent), name="add")

    def middle(value):
        return lax.ppermute(value, "expert", [(2, 4), (3, 5), (4, 2), (5, 3)])

    def ends(value):
        return lax.ppermute(value, "expert", [(4, 6), (5, 7), (2, 0), (3, 1)])

    def relay(value):
        pairs = [(0, 2), (1, 3), (2, 6), (3, 7), (4, 0), (5, 1), (6, 4), (7, 5)]
        return lax.ppermute(value, "expert", pairs)

    own_y = across(own)
    two = along(own, 2)
    one = along(own, 1)
    h0, d0, t0, s0 = back(*front(own, own_y))
    one_y = along(own_y, 1)
    q0 = add(t0, s0)
    two, one, q0 = lax.optimization_barrier((two, one, q0))
    inner = middle(after(own, two))
    outer = ends(two)
    two_y = across(two)
    h1, d1, t1, s1 = back(*front(one, one_y))
    q1 = add(t1, s1)
    inner, two_y, s1 = lax.optimization_barrier((inner, two_y, s1))
    inner_y = middle(after(own_y, inner))
    outer_y = ends(two_y)
    three = inner + outer
    three_y = inner_y + outer_y
    part2, swap2 = front(two, two_y)
    h2, d2, t2, s2 = back(after(part2, three, q1), swap2)
    q2 = add(t2, s2)
    got = relay(q2)
    h3, d3, t3, s3 = back(*front(after(three, q2), three_y))
    r1 = along(after(q1, s3), 1)
    q3 = call(last_kernel, struct(BLOCK, half, BF16), t3, across(s3), got, name="last")
    r3 = along(q3, 3)

    grads = call(
        grads_kernel,
        (struct(features, width, BF16), struct(features, width, BF16), struct(width, features, BF16)),
        after(own, q3), own_y, one, one_y, two, two_y, three, three_y, h0, h1, h2, h3, d0, d1, d2, d3,
        name="grads",
        out_specs=(pl.BlockSpec(memory_space=pltpu.HBM),) * 3,
        scratch_shapes=[
            pltpu.VMEM(w_gate.shape, BF16),
            pltpu.VMEM(w_up.shape, BF16),
            pltpu.VMEM(w_down.shape, BF16),
            pltpu.SemaphoreType.DMA((12,)),
        ],
    )
    grads, r1 = lax.optimization_barrier((grads, r1))
    near = call(near_kernel, struct(BLOCK, half, F32), q0, r1, got, name="near")
    grad_in = call(
        finish_kernel, struct(tokens.shape[0], features, BF16), placing_t, near, after(r3, near), name="finish"
    )
    return (grad_in,) + tuple(grads)


def solution(mesh):
    in_specs = (
        P(("pipe", "expert"), "tensor"),
        P(("pipe", "expert"), "tensor"),
        P(("pipe", "expert"), None),
        P(("pipe", "expert"), None),
        P("tensor", "expert"),
        P("tensor", "expert"),
        P("expert", "tensor"),
    )
    out_specs = (
        P(("pipe", "expert"), "tensor"),
        P(("pipe", "tensor"), "expert"),
        P(("pipe", "tensor"), "expert"),
        P(("pipe", "expert"), "tensor"),
    )
    small = mesh.shape["expert"] == 8 and mesh.shape["tensor"] == 2
    body = four_by_two if small else any_size
    return jax.shard_map(body, mesh=mesh, in_specs=in_specs, out_specs=out_specs, check_vma=False)
```

```python
import functools

import jax
import jax.numpy as jnp
from jax import lax
from jax.experimental import pallas as pl
from jax.experimental.pallas import tpu as pltpu
from jax.sharding import PartitionSpec as P

CAP = 36


window_expert = 0


def swiglu_grads(sums, width):
    z_gate = sums[:, :width]
    z_up = sums[:, width : 2 * width]
    d_hidden = sums[:, 2 * width :]
    sig = jax.nn.sigmoid(z_gate)
    act = z_gate * sig
    hidden = (act * z_up).astype(jnp.bfloat16)
    d_gate = (d_hidden * z_up * sig * (1.0 + z_gate * (1.0 - sig))).astype(jnp.bfloat16)
    d_up = (d_hidden * act).astype(jnp.bfloat16)
    return (hidden, jnp.concatenate([d_gate, d_up], axis=1))


def place(tokens, grad_out, expert_ids, gate_probs):
    chosen = expert_ids == window_expert
    weight = jnp.sum(jnp.where(chosen, gate_probs, jnp.zeros_like(gate_probs)), axis=1)
    scaled = (weight[:, None] * grad_out.astype(jnp.float32)).astype(jnp.bfloat16)
    routed = jnp.any(chosen, axis=1)
    slot_of = jnp.cumsum(routed.astype(jnp.int32)) - 1
    slot_ids = jnp.arange(CAP, dtype=jnp.int32)
    placing = ((slot_of[None, :] == slot_ids[:, None]) & routed[None, :]).astype(jnp.bfloat16)
    send_x = jnp.dot(placing, tokens, preferred_element_type=jnp.float32).astype(jnp.bfloat16)
    send_dy = jnp.dot(placing, scaled, preferred_element_type=jnp.float32).astype(jnp.bfloat16)
    return placing, send_x, send_dy


def unplace(placing, summed):
    return lax.dot_general(
        placing, summed, (((0,), (0,)), ((), ())), preferred_element_type=jnp.float32
    ).astype(jnp.bfloat16)


def weight_grads(rows_x, rows_dy, hidden, d_pre, width):
    grad_w_in = lax.dot_general(
        rows_x, d_pre, (((0,), (0,)), ((), ())), preferred_element_type=jnp.float32
    ).astype(jnp.bfloat16)
    grad_down = lax.dot_general(
        hidden, rows_dy, (((0,), (0,)), ((), ())), preferred_element_type=jnp.float32
    ).astype(jnp.bfloat16)
    return (grad_w_in[:, :width], grad_w_in[:, width:], grad_down)


def any_size(tokens, grad_out, expert_ids, gate_probs, w_gate, w_up, w_down):
    width = w_gate.shape[1]
    placing, send_x, send_dy = place(tokens, grad_out, expert_ids, gate_probs)
    rows_x, rows_dy = (
        lax.all_gather(send_x, "expert", axis=0, tiled=True),
        lax.all_gather(send_dy, "expert", axis=0, tiled=True),
    )
    w_in = jnp.concatenate([w_gate, w_up], axis=1)
    front = jnp.dot(rows_x, w_in, preferred_element_type=jnp.float32)
    back = lax.dot_general(
        rows_dy, w_down, (((1,), (1,)), ((), ())), preferred_element_type=jnp.float32
    )
    partial_value = jnp.concatenate([front, back], axis=1)
    share = lax.psum_scatter(
        partial_value.astype(jnp.bfloat16), "tensor", scatter_dimension=0, tiled=True
    ).astype(jnp.float32)
    hidden_part, grads_part = swiglu_grads(share, width)
    hidden, d_pre = (
        lax.all_gather(hidden_part, "tensor", axis=0, tiled=True),
        lax.all_gather(grads_part, "tensor", axis=0, tiled=True),
    )
    summed = lax.psum_scatter(
        lax.dot_general(
            d_pre, w_in, (((1,), (1,)), ((), ())), preferred_element_type=jnp.float32
        ).astype(jnp.bfloat16),
        "expert",
        scatter_dimension=0,
        tiled=True,
    )
    grad_in = unplace(placing, summed)
    return (grad_in,) + weight_grads(rows_x, rows_dy, hidden, d_pre, width)


MAIN = 32
TAIL = CAP - MAIN
BLOCK = 2 * CAP
TERM = 40
GROUP = 80
BF16, F32 = jnp.bfloat16, jnp.float32


def struct(rows, columns, dtype):
    return jax.ShapeDtypeStruct((rows, columns), dtype)


def call(kernel, outs, *args, name, **more):
    return pl.pallas_call(
        kernel,
        out_shape=outs,
        name=name,
        compiler_params=pltpu.CompilerParams(vmem_limit_bytes=24 * 2**20),
        cost_estimate=pl.CostEstimate(flops=1000, bytes_accessed=1000, transcendentals=0),
        **more,
    )(*args)


def mul(left, right, left_dim=1, right_dim=0):
    return lax.dot_general(
        left, right, (((left_dim,), (right_dim,)), ((), ())), preferred_element_type=F32
    )


def place_kernel(
    tokens_at, grad_out_at, ids_at, probs_at, block, placing_t, tokens, grad_out, ids, probs, done
):
    pairs = ((ids_at, ids), (probs_at, probs), (tokens_at, tokens), (grad_out_at, grad_out))
    copies = [pltpu.make_async_copy(a, b, done.at[i]) for i, (a, b) in enumerate(pairs)]
    for copy in copies:
        copy.start()
    rows = tokens.shape[0]
    copies[0].wait()
    copies[1].wait()
    chosen = ids[...] == window_expert
    weight_row = jnp.sum(jnp.where(chosen, probs[...], 0.0), axis=0, keepdims=True)
    routed_row = jnp.max(chosen.astype(F32), axis=0, keepdims=True)
    at_row = lax.broadcasted_iota(jnp.int32, (rows, rows), 0)
    at_column = lax.broadcasted_iota(jnp.int32, (rows, rows), 1)
    same = at_row == at_column
    routed = jnp.sum(jnp.where(same, routed_row, 0.0), axis=1, keepdims=True)
    slot_row = jnp.sum(jnp.where(at_row <= at_column, routed, 0.0), axis=0, keepdims=True) - 1.0
    slot = jnp.sum(jnp.where(at_column <= at_row, routed_row, 0.0), axis=1, keepdims=True) - 1.0
    wanted = lax.broadcasted_iota(jnp.int32, (TERM, rows), 0).astype(F32)
    placing = jnp.where((slot_row == wanted) & (routed_row > 0.0), 1.0, 0.0)
    wanted = at_column.astype(F32)
    placing_t[...] = jnp.where((slot == wanted) & (routed > 0.0), 1.0, 0.0).astype(BF16)
    scale = jnp.sum(placing * weight_row, axis=1, keepdims=True)
    placing = placing.astype(BF16)
    copies[2].wait()
    x = mul(placing, tokens[...])
    copies[3].wait()
    dy = mul(placing, grad_out[...]) * scale
    last = jnp.concatenate([x[MAIN:CAP], dy[MAIN:CAP]], axis=0)
    for at, value in ((0, x[0:MAIN]), (MAIN, dy[0:MAIN]), (2 * MAIN, last)):
        block[at : at + value.shape[0], :] = value.astype(BF16)


def tails(blocks, turned, columns):
    parts = []
    for block in blocks:
        last = block[2 * MAIN : BLOCK, columns].astype(F32)
        if turned:
            last = jnp.concatenate([last[TAIL:], last[:TAIL]], axis=0)
        parts.append(last)
    return jnp.concatenate(parts, axis=0).astype(BF16)


def rows_of(blocks, first, turned, columns):
    main = [block[first : first + MAIN, columns] for block in blocks]
    last = [tails(blocks[i : i + 2], turned, columns) for i in range(0, len(blocks), 2)]
    return jnp.concatenate(main + last, axis=0)


def front_kernel(mine, other, w_gate, w_up, w_down, part, sent):
    width = w_gate.shape[1]
    x = rows_of((mine, other), 0, False, slice(None))
    dy = rows_of((mine, other), MAIN, True, slice(None))
    for at, value in enumerate((mul(x, w_gate[...]), mul(x, w_up[...]), mul(dy, w_down[...], 1, 1))):
        part[:, at * width : (at + 1) * width] = value
        sent[:, at * width : (at + 1) * width] = value.astype(BF16)


def folded(main, last):
    half = main.shape[1] // 2
    return jnp.concatenate([main[:, :half], last[:, :half], main[:, half:], last[:, half:]], axis=0)


def back_kernel(part, arrived, w_gate, w_up, hidden, d_pre, term, *sent):
    width = w_gate.shape[1]
    sums = part[...] + arrived[...].astype(F32)
    z_gate, z_up, d_hidden = (sums[:, i * width : (i + 1) * width] for i in range(3))
    sig = jax.nn.sigmoid(z_gate)
    act = z_gate * sig
    row = lax.broadcasted_iota(jnp.int32, (GROUP, width), 0)
    real = (row < 2 * MAIN) | (row % 8 < TAIL)
    hidden[...] = jnp.where(real, act * z_up, 0.0).astype(BF16)
    d_gate = d_hidden * z_up * sig * (1.0 + z_gate * (1.0 - sig))
    d_gate = jnp.where(real, d_gate, 0.0).astype(BF16)
    d_up = jnp.where(real, d_hidden * act, 0.0).astype(BF16)
    d_pre[:, :width] = d_gate
    d_pre[:, width:] = d_up
    value = mul(d_gate, w_gate[...], 1, 1) + mul(d_up, w_up[...], 1, 1)
    term[...] = folded(value[0:MAIN], value[2 * MAIN : 2 * MAIN + TAIL])
    other = folded(value[MAIN : 2 * MAIN], value[2 * MAIN + 8 : 2 * MAIN + 8 + TAIL]).astype(BF16)
    at = 0
    for piece in sent:
        piece[...] = other[:, at : at + piece.shape[1]]
        at += piece.shape[1]


def add_kernel(term, arrived, total):
    total[...] = (term[...] + arrived[...].astype(F32)).astype(BF16)


def is_inner():
    line = lax.axis_index("expert") // 2
    return (line == 1) | (line == 2)


def last_kernel(start, term, arrived, passed, total):
    columns = slice(start, start + total.shape[1])
    value = term[:, columns] + arrived[...].astype(F32)
    total[...] = jnp.where(is_inner(), value + passed[:, columns].astype(F32), value).astype(BF16)


def near_kernel(first, second, passed, total):
    value = first[...].astype(F32) + second[...].astype(F32)
    total[...] = jnp.where(is_inner(), value, value + passed[...].astype(F32))


def finish_kernel(placing_t, near, left, right, grad_in):
    total = near[...] + jnp.concatenate([left[...], right[...]], axis=1).astype(F32)
    half = total.shape[1]
    placing = placing_t[:, :CAP]
    grad_in[:, :half] = mul(placing, total[:CAP].astype(BF16)).astype(BF16)
    grad_in[:, half:] = mul(placing, total[CAP:].astype(BF16)).astype(BF16)


def grads_kernel(*refs):
    blocks, hiddens, d_pres, outs, tiles, done = refs[:8], refs[8:12], refs[12:16], refs[16:19], refs[19:22], refs[22]
    features, width = outs[0].shape
    size = features // 4

    def groups(values):
        return jnp.concatenate(
            [v[: 2 * MAIN, :] for v in values] + [v[2 * MAIN :, :] for v in values], axis=0
        )

    d_pre, hidden = groups(d_pres), groups(hiddens)
    copies = []
    for step in range(4):
        at = slice(step * size, (step + 1) * size)
        x = rows_of(blocks, 0, False, at)
        tiles[0][at, :] = mul(x, d_pre[:, :width], 0, 0).astype(BF16)
        tiles[1][at, :] = mul(x, d_pre[:, width:], 0, 0).astype(BF16)
        tiles[2][:, at] = mul(hidden, rows_of(blocks, MAIN, True, at), 0, 0).astype(BF16)
        for i, place in enumerate(((at, slice(None)), (at, slice(None)), (slice(None), at))):
            copy = pltpu.make_async_copy(tiles[i].at[place], outs[i].at[place], done.at[3 * step + i])
            copy.start()
            copies.append(copy)
    for copy in copies:
        copy.wait()


def load_kernel(*refs):
    copies = [pltpu.make_async_copy(refs[i], refs[3 + i], refs[6].at[i]) for i in range(3)]
    for copy in copies:
        copy.start()
    for copy in copies:
        copy.wait()


def four_by_two(tokens, grad_out, expert_ids, gate_probs, w_gate, w_up, w_down):
    features, width = w_gate.shape
    half = features // 2
    in_hbm = pl.BlockSpec(memory_space=pltpu.HBM)

    def across(value):
        return lax.ppermute(value, "expert", [(i, i ^ 1) for i in range(8)])

    def along(value, distance):
        return lax.ppermute(value, "expert", [(i, i ^ (2 * distance)) for i in range(8)])

    def after(value, *others):
        return lax.optimization_barrier((value,) + others)[0]

    def hbm(value):
        return pltpu.with_memory_space_constraint(value, pltpu.HBM)

    own, placing_t = call(
        place_kernel,
        (
            struct(BLOCK, features, BF16),
            struct(tokens.shape[0], tokens.shape[0], BF16),
        ),
        hbm(tokens), hbm(grad_out), hbm(expert_ids.T), hbm(gate_probs.T), name="place",
        in_specs=[in_hbm] * 4,
        scratch_shapes=[
            pltpu.VMEM(tokens.shape, BF16),
            pltpu.VMEM(tokens.shape, BF16),
            pltpu.VMEM(expert_ids.shape[::-1], jnp.int32),
            pltpu.VMEM(gate_probs.shape[::-1], F32),
            pltpu.SemaphoreType.DMA((4,)),
        ],
    )
    w_gate, w_up, w_down, _ = lax.optimization_barrier((w_gate, w_up, w_down, own))
    gate, up, down = call(
        load_kernel,
        tuple(struct(*w.shape, BF16) for w in (w_gate, w_up, w_down)),
        hbm(w_gate), hbm(w_up), hbm(w_down), name="load",
        in_specs=[in_hbm] * 3,
        scratch_shapes=[pltpu.SemaphoreType.DMA((3,))],
    )

    def front(mine, other):
        part, sent = call(
            front_kernel,
            (struct(GROUP, 3 * width, F32), struct(GROUP, 3 * width, BF16)),
            mine, other, gate, up, down, name="front",
        )
        return part, lax.ppermute(sent, "tensor", [(0, 1), (1, 0)])

    def back(part, arrived, *pieces):
        return call(
            back_kernel,
            (struct(GROUP, width, BF16), struct(GROUP, 2 * width, BF16), struct(BLOCK, half, F32))
            + tuple(struct(BLOCK, size, BF16) for size in pieces or (half,)),
            part, arrived, gate, up, name="back",
        )

    def add(term, sent):
        return call(add_kernel, struct(BLOCK, half, BF16), term, across(sent), name="add")

    def middle(value):
        return lax.ppermute(value, "expert", [(2, 4), (3, 5), (4, 2), (5, 3)])

    def ends(value):
        return lax.ppermute(value, "expert", [(4, 6), (5, 7), (2, 0), (3, 1)])

    def relay(value):
        pairs = [(0, 2), (1, 3), (2, 6), (3, 7), (4, 0), (5, 1), (6, 4), (7, 5)]
        return lax.ppermute(value, "expert", pairs)

    own_y = across(own)
    two = along(own, 2)
    one = along(own, 1)
    h0, d0, t0, s0 = back(*front(own, own_y))
    one_y = along(own_y, 1)
    q0 = add(t0, s0)
    two, one, q0 = lax.optimization_barrier((two, one, q0))
    two_y = across(two)
    outer = ends(two)
    inner = middle(after(own, two))
    h1, d1, t1, s1 = back(*front(one, one_y))
    q1 = add(t1, s1)
    inner, two_y, s1 = lax.optimization_barrier((inner, two_y, s1))
    outer_y = ends(two_y)
    inner_y = middle(after(own_y, inner))
    three = inner + outer
    three_y = inner_y + outer_y
    part2, swap2 = front(two, two_y)
    h2, d2, t2, s2 = back(after(part2, three), swap2)
    q2 = add(t2, after(s2, q1))
    got = relay(q2)
    large = half * 2 // 3
    h3, d3, t3, *s3 = back(*front(three, three_y), large, half - large)
    r1 = along(after(q1, *s3), 1)
    q3 = [
        call(
            functools.partial(last_kernel, at), struct(*value.shape, BF16),
            t3, across(value), got, name="last",
        )
        for at, value in zip((0, large), s3)
    ]
    r3 = [along(value, 3) for value in q3]

    grads = call(
        grads_kernel,
        (struct(features, width, BF16), struct(features, width, BF16), struct(width, features, BF16)),
        after(own, q3[1]), own_y, one, one_y, two, two_y, three, three_y, h0, h1, h2, h3, d0, d1, d2, d3,
        name="grads",
        out_specs=(pl.BlockSpec(memory_space=pltpu.HBM),) * 3,
        scratch_shapes=[
            pltpu.VMEM(w_gate.shape, BF16),
            pltpu.VMEM(w_up.shape, BF16),
            pltpu.VMEM(w_down.shape, BF16),
            pltpu.SemaphoreType.DMA((12,)),
        ],
    )
    grads, r1 = lax.optimization_barrier((grads, r1))
    near = call(near_kernel, struct(BLOCK, half, F32), q0, r1, got, name="near")
    grad_in = call(
        finish_kernel, struct(tokens.shape[0], features, BF16), placing_t, near, *after(r3, near), name="finish"
    )
    return (grad_in,) + tuple(grads)


def solution(mesh):
    in_specs = (
        P(("pipe", "expert"), "tensor"),
        P(("pipe", "expert"), "tensor"),
        P(("pipe", "expert"), None),
        P(("pipe", "expert"), None),
        P("tensor", "expert"),
        P("tensor", "expert"),
        P("expert", "tensor"),
    )
    out_specs = (
        P(("pipe", "expert"), "tensor"),
        P(("pipe", "tensor"), "expert"),
        P(("pipe", "tensor"), "expert"),
        P(("pipe", "expert"), "tensor"),
    )
    small = mesh.shape["expert"] == 8 and mesh.shape["tensor"] == 2
    body = four_by_two if small else any_size
    return jax.shard_map(body, mesh=mesh, in_specs=in_specs, out_specs=out_specs, check_vma=False)
```

```python
import functools

import jax
import jax.numpy as jnp
from jax import lax
from jax.experimental import pallas as pl
from jax.experimental.pallas import tpu as pltpu
from jax.sharding import PartitionSpec as P

CAP = 36


window_expert = 0


def swiglu_grads(sums, width):
    z_gate = sums[:, :width]
    z_up = sums[:, width : 2 * width]
    d_hidden = sums[:, 2 * width :]
    sig = jax.nn.sigmoid(z_gate)
    act = z_gate * sig
    hidden = (act * z_up).astype(jnp.bfloat16)
    d_gate = (d_hidden * z_up * sig * (1.0 + z_gate * (1.0 - sig))).astype(jnp.bfloat16)
    d_up = (d_hidden * act).astype(jnp.bfloat16)
    return (hidden, jnp.concatenate([d_gate, d_up], axis=1))


def place(tokens, grad_out, expert_ids, gate_probs):
    chosen = expert_ids == window_expert
    weight = jnp.sum(jnp.where(chosen, gate_probs, jnp.zeros_like(gate_probs)), axis=1)
    scaled = (weight[:, None] * grad_out.astype(jnp.float32)).astype(jnp.bfloat16)
    routed = jnp.any(chosen, axis=1)
    slot_of = jnp.cumsum(routed.astype(jnp.int32)) - 1
    slot_ids = jnp.arange(CAP, dtype=jnp.int32)
    placing = ((slot_of[None, :] == slot_ids[:, None]) & routed[None, :]).astype(jnp.bfloat16)
    send_x = jnp.dot(placing, tokens, preferred_element_type=jnp.float32).astype(jnp.bfloat16)
    send_dy = jnp.dot(placing, scaled, preferred_element_type=jnp.float32).astype(jnp.bfloat16)
    return placing, send_x, send_dy


def unplace(placing, summed):
    return lax.dot_general(
        placing, summed, (((0,), (0,)), ((), ())), preferred_element_type=jnp.float32
    ).astype(jnp.bfloat16)


def weight_grads(rows_x, rows_dy, hidden, d_pre, width):
    grad_w_in = lax.dot_general(
        rows_x, d_pre, (((0,), (0,)), ((), ())), preferred_element_type=jnp.float32
    ).astype(jnp.bfloat16)
    grad_down = lax.dot_general(
        hidden, rows_dy, (((0,), (0,)), ((), ())), preferred_element_type=jnp.float32
    ).astype(jnp.bfloat16)
    return (grad_w_in[:, :width], grad_w_in[:, width:], grad_down)


def any_size(tokens, grad_out, expert_ids, gate_probs, w_gate, w_up, w_down):
    width = w_gate.shape[1]
    placing, send_x, send_dy = place(tokens, grad_out, expert_ids, gate_probs)
    rows_x, rows_dy = (
        lax.all_gather(send_x, "expert", axis=0, tiled=True),
        lax.all_gather(send_dy, "expert", axis=0, tiled=True),
    )
    w_in = jnp.concatenate([w_gate, w_up], axis=1)
    front = jnp.dot(rows_x, w_in, preferred_element_type=jnp.float32)
    back = lax.dot_general(
        rows_dy, w_down, (((1,), (1,)), ((), ())), preferred_element_type=jnp.float32
    )
    partial_value = jnp.concatenate([front, back], axis=1)
    share = lax.psum_scatter(
        partial_value.astype(jnp.bfloat16), "tensor", scatter_dimension=0, tiled=True
    ).astype(jnp.float32)
    hidden_part, grads_part = swiglu_grads(share, width)
    hidden, d_pre = (
        lax.all_gather(hidden_part, "tensor", axis=0, tiled=True),
        lax.all_gather(grads_part, "tensor", axis=0, tiled=True),
    )
    summed = lax.psum_scatter(
        lax.dot_general(
            d_pre, w_in, (((1,), (1,)), ((), ())), preferred_element_type=jnp.float32
        ).astype(jnp.bfloat16),
        "expert",
        scatter_dimension=0,
        tiled=True,
    )
    grad_in = unplace(placing, summed)
    return (grad_in,) + weight_grads(rows_x, rows_dy, hidden, d_pre, width)


MAIN = 32
TAIL = CAP - MAIN
BLOCK = 2 * CAP
TERM = 40
GROUP = 80
BF16, F32 = jnp.bfloat16, jnp.float32


def struct(rows, columns, dtype):
    return jax.ShapeDtypeStruct((rows, columns), dtype)


def call(kernel, outs, *args, name, **more):
    return pl.pallas_call(
        kernel,
        out_shape=outs,
        name=name,
        compiler_params=pltpu.CompilerParams(vmem_limit_bytes=24 * 2**20),
        cost_estimate=pl.CostEstimate(flops=1000, bytes_accessed=1000, transcendentals=0),
        **more,
    )(*args)


def mul(left, right, left_dim=1, right_dim=0):
    return lax.dot_general(
        left, right, (((left_dim,), (right_dim,)), ((), ())), preferred_element_type=F32
    )


def place_kernel(
    tokens_at, grad_out_at, ids_at, probs_at, block, placing_t, tokens, grad_out, ids, probs, done
):
    pairs = ((ids_at, ids), (probs_at, probs), (tokens_at, tokens), (grad_out_at, grad_out))
    copies = [pltpu.make_async_copy(a, b, done.at[i]) for i, (a, b) in enumerate(pairs)]
    for copy in copies:
        copy.start()
    rows = tokens.shape[0]
    copies[0].wait()
    copies[1].wait()
    chosen = ids[...] == window_expert
    weight_row = jnp.sum(jnp.where(chosen, probs[...], 0.0), axis=0, keepdims=True)
    routed_row = jnp.max(chosen.astype(F32), axis=0, keepdims=True)
    at_row = lax.broadcasted_iota(jnp.int32, (rows, rows), 0)
    at_column = lax.broadcasted_iota(jnp.int32, (rows, rows), 1)
    same = at_row == at_column
    routed = jnp.sum(jnp.where(same, routed_row, 0.0), axis=1, keepdims=True)
    slot_row = jnp.sum(jnp.where(at_row <= at_column, routed, 0.0), axis=0, keepdims=True) - 1.0
    slot = jnp.sum(jnp.where(at_column <= at_row, routed_row, 0.0), axis=1, keepdims=True) - 1.0
    wanted = lax.broadcasted_iota(jnp.int32, (TERM, rows), 0).astype(F32)
    placing = jnp.where((slot_row == wanted) & (routed_row > 0.0), 1.0, 0.0)
    wanted = at_column.astype(F32)
    placing_t[...] = jnp.where((slot == wanted) & (routed > 0.0), 1.0, 0.0).astype(BF16)
    scale = jnp.sum(placing * weight_row, axis=1, keepdims=True)
    placing = placing.astype(BF16)
    copies[2].wait()
    x = mul(placing, tokens[...])
    copies[3].wait()
    dy = mul(placing, grad_out[...]) * scale
    last = jnp.concatenate([x[MAIN:CAP], dy[MAIN:CAP]], axis=0)
    for at, value in ((0, x[0:MAIN]), (MAIN, dy[0:MAIN]), (2 * MAIN, last)):
        block[at : at + value.shape[0], :] = value.astype(BF16)


def tails(blocks, turned, columns):
    parts = []
    for block in blocks:
        last = block[2 * MAIN : BLOCK, columns].astype(F32)
        if turned:
            last = jnp.concatenate([last[TAIL:], last[:TAIL]], axis=0)
        parts.append(last)
    return jnp.concatenate(parts, axis=0).astype(BF16)


def rows_of(blocks, first, turned, columns):
    main = [block[first : first + MAIN, columns] for block in blocks]
    last = [tails(blocks[i : i + 2], turned, columns) for i in range(0, len(blocks), 2)]
    return jnp.concatenate(main + last, axis=0)


def front_kernel(mine, other, w_gate, w_up, w_down, part, sent):
    width = w_gate.shape[1]
    x = rows_of((mine, other), 0, False, slice(None))
    dy = rows_of((mine, other), MAIN, True, slice(None))
    for at, value in enumerate((mul(x, w_gate[...]), mul(x, w_up[...]), mul(dy, w_down[...], 1, 1))):
        part[:, at * width : (at + 1) * width] = value
        sent[:, at * width : (at + 1) * width] = value.astype(BF16)


def folded(main, last):
    half = main.shape[1] // 2
    return jnp.concatenate([main[:, :half], last[:, :half], main[:, half:], last[:, half:]], axis=0)


def back_kernel(part, arrived, w_gate, w_up, hidden, d_pre, term, *sent):
    width = w_gate.shape[1]
    sums = part[...] + arrived[...].astype(F32)
    z_gate, z_up, d_hidden = (sums[:, i * width : (i + 1) * width] for i in range(3))
    sig = jax.nn.sigmoid(z_gate)
    act = z_gate * sig
    row = lax.broadcasted_iota(jnp.int32, (GROUP, width), 0)
    real = (row < 2 * MAIN) | (row % 8 < TAIL)
    hidden[...] = jnp.where(real, act * z_up, 0.0).astype(BF16)
    d_gate = d_hidden * z_up * sig * (1.0 + z_gate * (1.0 - sig))
    d_gate = jnp.where(real, d_gate, 0.0).astype(BF16)
    d_up = jnp.where(real, d_hidden * act, 0.0).astype(BF16)
    d_pre[:, :width] = d_gate
    d_pre[:, width:] = d_up
    value = mul(d_gate, w_gate[...], 1, 1) + mul(d_up, w_up[...], 1, 1)
    term[...] = folded(value[0:MAIN], value[2 * MAIN : 2 * MAIN + TAIL])
    other = folded(value[MAIN : 2 * MAIN], value[2 * MAIN + 8 : 2 * MAIN + 8 + TAIL]).astype(BF16)
    at = 0
    for piece in sent:
        piece[...] = other[:, at : at + piece.shape[1]]
        at += piece.shape[1]


def pair_kernel(left, right, out):
    width = left.shape[1]
    out[:, :width] = left[...]
    out[:, width:] = right[...]


def split_kernel(inner, outer, outer_y, block, block_y):
    width = block.shape[1]
    block[...] = inner[:, :width] + outer[...]
    block_y[...] = inner[:, width:] + outer_y[...]


def add_kernel(term, arrived, total):
    total[...] = (term[...] + arrived[...].astype(F32)).astype(BF16)


def is_inner():
    line = lax.axis_index("expert") // 2
    return (line == 1) | (line == 2)


def last_kernel(start, term, arrived, passed, total):
    columns = slice(start, start + total.shape[1])
    value = term[:, columns] + arrived[...].astype(F32)
    total[...] = jnp.where(is_inner(), value + passed[:, columns].astype(F32), value).astype(BF16)


def near_kernel(first, second, passed, total):
    value = first[...].astype(F32) + second[...].astype(F32)
    total[...] = jnp.where(is_inner(), value, value + passed[...].astype(F32))


def finish_kernel(placing_t, near, left, right, grad_in):
    total = near[...] + jnp.concatenate([left[...], right[...]], axis=1).astype(F32)
    half = total.shape[1]
    placing = placing_t[:, :CAP]
    grad_in[:, :half] = mul(placing, total[:CAP].astype(BF16)).astype(BF16)
    grad_in[:, half:] = mul(placing, total[CAP:].astype(BF16)).astype(BF16)


def grads_kernel(*refs):
    blocks, hiddens, d_pres, outs, tiles, done = refs[:8], refs[8:12], refs[12:16], refs[16:19], refs[19:22], refs[22]
    features, width = outs[0].shape
    size = features // 4

    def groups(values):
        return jnp.concatenate(
            [v[: 2 * MAIN, :] for v in values] + [v[2 * MAIN :, :] for v in values], axis=0
        )

    d_pre, hidden = groups(d_pres), groups(hiddens)
    copies = []
    for step in range(4):
        at = slice(step * size, (step + 1) * size)
        x = rows_of(blocks, 0, False, at)
        tiles[0][at, :] = mul(x, d_pre[:, :width], 0, 0).astype(BF16)
        tiles[1][at, :] = mul(x, d_pre[:, width:], 0, 0).astype(BF16)
        tiles[2][:, at] = mul(hidden, rows_of(blocks, MAIN, True, at), 0, 0).astype(BF16)
        for i, place in enumerate(((at, slice(None)), (at, slice(None)), (slice(None), at))):
            copy = pltpu.make_async_copy(tiles[i].at[place], outs[i].at[place], done.at[3 * step + i])
            copy.start()
            copies.append(copy)
    for copy in copies:
        copy.wait()


def load_kernel(*refs):
    copies = [pltpu.make_async_copy(refs[i], refs[3 + i], refs[6].at[i]) for i in range(3)]
    for copy in copies:
        copy.start()
    for copy in copies:
        copy.wait()


def four_by_two(tokens, grad_out, expert_ids, gate_probs, w_gate, w_up, w_down):
    features, width = w_gate.shape
    half = features // 2
    in_hbm = pl.BlockSpec(memory_space=pltpu.HBM)

    def across(value):
        return lax.ppermute(value, "expert", [(i, i ^ 1) for i in range(8)])

    def along(value, distance):
        return lax.ppermute(value, "expert", [(i, i ^ (2 * distance)) for i in range(8)])

    def after(value, *others):
        return lax.optimization_barrier((value,) + others)[0]

    def hbm(value):
        return pltpu.with_memory_space_constraint(value, pltpu.HBM)

    own, placing_t = call(
        place_kernel,
        (
            struct(BLOCK, features, BF16),
            struct(tokens.shape[0], tokens.shape[0], BF16),
        ),
        hbm(tokens), hbm(grad_out), hbm(expert_ids.T), hbm(gate_probs.T), name="place",
        in_specs=[in_hbm] * 4,
        scratch_shapes=[
            pltpu.VMEM(tokens.shape, BF16),
            pltpu.VMEM(tokens.shape, BF16),
            pltpu.VMEM(expert_ids.shape[::-1], jnp.int32),
            pltpu.VMEM(gate_probs.shape[::-1], F32),
            pltpu.SemaphoreType.DMA((4,)),
        ],
    )
    w_gate, w_up, w_down, _ = lax.optimization_barrier((w_gate, w_up, w_down, own))
    gate, up, down = call(
        load_kernel,
        tuple(struct(*w.shape, BF16) for w in (w_gate, w_up, w_down)),
        hbm(w_gate), hbm(w_up), hbm(w_down), name="load",
        in_specs=[in_hbm] * 3,
        scratch_shapes=[pltpu.SemaphoreType.DMA((3,))],
    )

    def front(mine, other):
        part, sent = call(
            front_kernel,
            (struct(GROUP, 3 * width, F32), struct(GROUP, 3 * width, BF16)),
            mine, other, gate, up, down, name="front",
        )
        return part, lax.ppermute(sent, "tensor", [(0, 1), (1, 0)])

    def back(part, arrived, *pieces):
        return call(
            back_kernel,
            (struct(GROUP, width, BF16), struct(GROUP, 2 * width, BF16), struct(BLOCK, half, F32))
            + tuple(struct(BLOCK, size, BF16) for size in pieces or (half,)),
            part, arrived, gate, up, name="back",
        )

    def add(term, sent):
        return call(add_kernel, struct(BLOCK, half, BF16), term, across(sent), name="add")

    def middle(value):
        return lax.ppermute(value, "expert", [(2, 4), (3, 5), (4, 2), (5, 3)])

    def ends(value):
        return lax.ppermute(value, "expert", [(4, 6), (5, 7), (2, 0), (3, 1)])

    def relay(value):
        pairs = [(0, 2), (1, 3), (2, 6), (3, 7), (4, 0), (5, 1), (6, 4), (7, 5)]
        return lax.ppermute(value, "expert", pairs)

    own_y = across(own)
    two = along(own, 2)
    one = along(own, 1)
    h0, d0, t0, s0 = back(*front(own, own_y))
    one_y = along(own_y, 1)
    pair = call(pair_kernel, struct(BLOCK, 2 * features, BF16), own, own_y, name="pair")
    q0 = add(t0, s0)
    two, one, q0, pair = lax.optimization_barrier((two, one, q0, pair))
    inner = middle(after(pair, two))
    outer = ends(two)
    two_y = across(two)
    h1, d1, t1, s1 = back(*front(one, one_y))
    q1 = add(t1, s1)
    two_y, s1 = lax.optimization_barrier((two_y, s1))
    outer_y = ends(two_y)
    part2, swap2 = front(two, two_y)
    h2, d2, t2, s2 = back(after(part2, outer, q1), swap2)
    q2 = add(t2, s2)
    got = relay(q2)
    large = half * 2 // 3
    three, three_y = call(
        split_kernel, (struct(BLOCK, features, BF16),) * 2, inner, outer, outer_y, name="split"
    )
    h3, d3, t3, *s3 = back(*front(three, three_y), large, half - large)
    r1 = along(after(q1, *s3), 1)
    q3 = [
        call(
            functools.partial(last_kernel, at), struct(*value.shape, BF16),
            t3, across(value), got, name="last",
        )
        for at, value in zip((0, large), s3)
    ]
    r3 = [along(value, 3) for value in q3]

    grads = call(
        grads_kernel,
        (struct(features, width, BF16), struct(features, width, BF16), struct(width, features, BF16)),
        after(own, q3[1]), own_y, one, one_y, two, two_y, three, three_y, h0, h1, h2, h3, d0, d1, d2, d3,
        name="grads",
        out_specs=(pl.BlockSpec(memory_space=pltpu.HBM),) * 3,
        scratch_shapes=[
            pltpu.VMEM(w_gate.shape, BF16),
            pltpu.VMEM(w_up.shape, BF16),
            pltpu.VMEM(w_down.shape, BF16),
            pltpu.SemaphoreType.DMA((12,)),
        ],
    )
    grads, r1 = lax.optimization_barrier((grads, r1))
    near = call(near_kernel, struct(BLOCK, half, F32), q0, r1, got, name="near")
    grad_in = call(
        finish_kernel, struct(tokens.shape[0], features, BF16), placing_t, near, *after(r3, near), name="finish"
    )
    return (grad_in,) + tuple(grads)


def solution(mesh):
    in_specs = (
        P(("pipe", "expert"), "tensor"),
        P(("pipe", "expert"), "tensor"),
        P(("pipe", "expert"), None),
        P(("pipe", "expert"), None),
        P("tensor", "expert"),
        P("tensor", "expert"),
        P("expert", "tensor"),
    )
    out_specs = (
        P(("pipe", "expert"), "tensor"),
        P(("pipe", "tensor"), "expert"),
        P(("pipe", "tensor"), "expert"),
        P(("pipe", "expert"), "tensor"),
    )
    small = mesh.shape["expert"] == 8 and mesh.shape["tensor"] == 2
    body = four_by_two if small else any_size
    return jax.shard_map(body, mesh=mesh, in_specs=in_specs, out_specs=out_specs, check_vma=False)
```

```python
import functools

import jax
import jax.numpy as jnp
from jax import lax
from jax.experimental import pallas as pl
from jax.experimental.pallas import tpu as pltpu
from jax.sharding import PartitionSpec as P

CAP = 36


window_expert = 0


def swiglu_grads(sums, width):
    z_gate = sums[:, :width]
    z_up = sums[:, width : 2 * width]
    d_hidden = sums[:, 2 * width :]
    sig = jax.nn.sigmoid(z_gate)
    act = z_gate * sig
    hidden = (act * z_up).astype(jnp.bfloat16)
    d_gate = (d_hidden * z_up * sig * (1.0 + z_gate * (1.0 - sig))).astype(jnp.bfloat16)
    d_up = (d_hidden * act).astype(jnp.bfloat16)
    return (hidden, jnp.concatenate([d_gate, d_up], axis=1))


def place(tokens, grad_out, expert_ids, gate_probs):
    chosen = expert_ids == window_expert
    weight = jnp.sum(jnp.where(chosen, gate_probs, jnp.zeros_like(gate_probs)), axis=1)
    scaled = (weight[:, None] * grad_out.astype(jnp.float32)).astype(jnp.bfloat16)
    routed = jnp.any(chosen, axis=1)
    slot_of = jnp.cumsum(routed.astype(jnp.int32)) - 1
    slot_ids = jnp.arange(CAP, dtype=jnp.int32)
    placing = ((slot_of[None, :] == slot_ids[:, None]) & routed[None, :]).astype(jnp.bfloat16)
    send_x = jnp.dot(placing, tokens, preferred_element_type=jnp.float32).astype(jnp.bfloat16)
    send_dy = jnp.dot(placing, scaled, preferred_element_type=jnp.float32).astype(jnp.bfloat16)
    return placing, send_x, send_dy


def unplace(placing, summed):
    return lax.dot_general(
        placing, summed, (((0,), (0,)), ((), ())), preferred_element_type=jnp.float32
    ).astype(jnp.bfloat16)


def weight_grads(rows_x, rows_dy, hidden, d_pre, width):
    grad_w_in = lax.dot_general(
        rows_x, d_pre, (((0,), (0,)), ((), ())), preferred_element_type=jnp.float32
    ).astype(jnp.bfloat16)
    grad_down = lax.dot_general(
        hidden, rows_dy, (((0,), (0,)), ((), ())), preferred_element_type=jnp.float32
    ).astype(jnp.bfloat16)
    return (grad_w_in[:, :width], grad_w_in[:, width:], grad_down)


def any_size(tokens, grad_out, expert_ids, gate_probs, w_gate, w_up, w_down):
    width = w_gate.shape[1]
    placing, send_x, send_dy = place(tokens, grad_out, expert_ids, gate_probs)
    rows_x, rows_dy = (
        lax.all_gather(send_x, "expert", axis=0, tiled=True),
        lax.all_gather(send_dy, "expert", axis=0, tiled=True),
    )
    w_in = jnp.concatenate([w_gate, w_up], axis=1)
    front = jnp.dot(rows_x, w_in, preferred_element_type=jnp.float32)
    back = lax.dot_general(
        rows_dy, w_down, (((1,), (1,)), ((), ())), preferred_element_type=jnp.float32
    )
    partial_value = jnp.concatenate([front, back], axis=1)
    share = lax.psum_scatter(
        partial_value.astype(jnp.bfloat16), "tensor", scatter_dimension=0, tiled=True
    ).astype(jnp.float32)
    hidden_part, grads_part = swiglu_grads(share, width)
    hidden, d_pre = (
        lax.all_gather(hidden_part, "tensor", axis=0, tiled=True),
        lax.all_gather(grads_part, "tensor", axis=0, tiled=True),
    )
    summed = lax.psum_scatter(
        lax.dot_general(
            d_pre, w_in, (((1,), (1,)), ((), ())), preferred_element_type=jnp.float32
        ).astype(jnp.bfloat16),
        "expert",
        scatter_dimension=0,
        tiled=True,
    )
    grad_in = unplace(placing, summed)
    return (grad_in,) + weight_grads(rows_x, rows_dy, hidden, d_pre, width)


MAIN = 32
TAIL = CAP - MAIN
BLOCK = 2 * CAP
TERM = 40
GROUP = 80
BF16, F32 = jnp.bfloat16, jnp.float32


def struct(rows, columns, dtype):
    return jax.ShapeDtypeStruct((rows, columns), dtype)


def call(kernel, outs, *args, name, **more):
    return pl.pallas_call(
        kernel,
        out_shape=outs,
        name=name,
        compiler_params=pltpu.CompilerParams(vmem_limit_bytes=24 * 2**20),
        cost_estimate=pl.CostEstimate(flops=1000, bytes_accessed=1000, transcendentals=0),
        **more,
    )(*args)


def mul(left, right, left_dim=1, right_dim=0):
    return lax.dot_general(
        left, right, (((left_dim,), (right_dim,)), ((), ())), preferred_element_type=F32
    )


def place_kernel(
    tokens_at, grad_out_at, ids_at, probs_at, block, placing_t, tokens, grad_out, ids, probs, done
):
    pairs = ((ids_at, ids), (probs_at, probs), (tokens_at, tokens), (grad_out_at, grad_out))
    copies = [pltpu.make_async_copy(a, b, done.at[i]) for i, (a, b) in enumerate(pairs)]
    for copy in copies:
        copy.start()
    rows = tokens.shape[0]
    copies[0].wait()
    copies[1].wait()
    chosen = ids[...] == window_expert
    weight_row = jnp.sum(jnp.where(chosen, probs[...], 0.0), axis=0, keepdims=True)
    routed_row = jnp.max(chosen.astype(F32), axis=0, keepdims=True)
    at_row = lax.broadcasted_iota(jnp.int32, (rows, rows), 0)
    at_column = lax.broadcasted_iota(jnp.int32, (rows, rows), 1)
    same = at_row == at_column
    routed = jnp.sum(jnp.where(same, routed_row, 0.0), axis=1, keepdims=True)
    slot_row = jnp.sum(jnp.where(at_row <= at_column, routed, 0.0), axis=0, keepdims=True) - 1.0
    slot = jnp.sum(jnp.where(at_column <= at_row, routed_row, 0.0), axis=1, keepdims=True) - 1.0
    wanted = lax.broadcasted_iota(jnp.int32, (TERM, rows), 0).astype(F32)
    placing = jnp.where((slot_row == wanted) & (routed_row > 0.0), 1.0, 0.0)
    wanted = at_column.astype(F32)
    placing_t[...] = jnp.where((slot == wanted) & (routed > 0.0), 1.0, 0.0).astype(BF16)
    scale = jnp.sum(placing * weight_row, axis=1, keepdims=True)
    placing = placing.astype(BF16)
    copies[2].wait()
    x = mul(placing, tokens[...])
    copies[3].wait()
    dy = mul(placing, grad_out[...]) * scale
    last = jnp.concatenate([x[MAIN:CAP], dy[MAIN:CAP]], axis=0)
    for at, value in ((0, x[0:MAIN]), (MAIN, dy[0:MAIN]), (2 * MAIN, last)):
        block[at : at + value.shape[0], :] = value.astype(BF16)


def tails(blocks, turned, columns):
    parts = []
    for block in blocks:
        last = block[2 * MAIN : BLOCK, columns].astype(F32)
        if turned:
            last = jnp.concatenate([last[TAIL:], last[:TAIL]], axis=0)
        parts.append(last)
    return jnp.concatenate(parts, axis=0).astype(BF16)


def rows_of(blocks, first, turned, columns):
    main = [block[first : first + MAIN, columns] for block in blocks]
    last = [tails(blocks[i : i + 2], turned, columns) for i in range(0, len(blocks), 2)]
    return jnp.concatenate(main + last, axis=0)


def front_kernel(mine, other, w_gate, w_up, w_down, part, sent):
    width = w_gate.shape[1]
    x = rows_of((mine, other), 0, False, slice(None))
    dy = rows_of((mine, other), MAIN, True, slice(None))
    for at, value in enumerate((mul(x, w_gate[...]), mul(x, w_up[...]), mul(dy, w_down[...], 1, 1))):
        part[:, at * width : (at + 1) * width] = value
        sent[:, at * width : (at + 1) * width] = value.astype(BF16)


def folded(main, last):
    half = main.shape[1] // 2
    return jnp.concatenate([main[:, :half], last[:, :half], main[:, half:], last[:, half:]], axis=0)


def back_kernel(part, arrived, w_gate, w_up, hidden, d_pre, term, *sent):
    width = w_gate.shape[1]
    sums = part[...] + arrived[...].astype(F32)
    z_gate, z_up, d_hidden = (sums[:, i * width : (i + 1) * width] for i in range(3))
    sig = jax.nn.sigmoid(z_gate)
    act = z_gate * sig
    row = lax.broadcasted_iota(jnp.int32, (GROUP, width), 0)
    real = (row < 2 * MAIN) | (row % 8 < TAIL)
    hidden[...] = jnp.where(real, act * z_up, 0.0).astype(BF16)
    d_gate = d_hidden * z_up * sig * (1.0 + z_gate * (1.0 - sig))
    d_gate = jnp.where(real, d_gate, 0.0).astype(BF16)
    d_up = jnp.where(real, d_hidden * act, 0.0).astype(BF16)
    d_pre[:, :width] = d_gate
    d_pre[:, width:] = d_up
    value = mul(d_gate, w_gate[...], 1, 1) + mul(d_up, w_up[...], 1, 1)
    term[...] = folded(value[0:MAIN], value[2 * MAIN : 2 * MAIN + TAIL])
    other = folded(value[MAIN : 2 * MAIN], value[2 * MAIN + 8 : 2 * MAIN + 8 + TAIL]).astype(BF16)
    at = 0
    for piece in sent:
        piece[...] = other[:, at : at + piece.shape[1]]
        at += piece.shape[1]


def pair_kernel(left, right, out):
    width = left.shape[1]
    out[:, :width] = left[...]
    out[:, width:] = right[...]


def split_kernel(inner, outer, outer_y, block, block_y):
    width = block.shape[1]
    block[...] = inner[:, :width] + outer[...]
    block_y[...] = inner[:, width:] + outer_y[...]


def add_kernel(term, arrived, total):
    total[...] = (term[...] + arrived[...].astype(F32)).astype(BF16)


def is_inner():
    line = lax.axis_index("expert") // 2
    return (line == 1) | (line == 2)


def last_kernel(start, term, arrived, passed, total):
    columns = slice(start, start + total.shape[1])
    value = term[:, columns] + arrived[...].astype(F32)
    total[...] = jnp.where(is_inner(), value + passed[:, columns].astype(F32), value).astype(BF16)


def near_kernel(first, second, passed, total):
    value = first[...].astype(F32) + second[...].astype(F32)
    total[...] = jnp.where(is_inner(), value, value + passed[...].astype(F32))


def finish_kernel(placing_t, near, left, right, grad_in, tile, done):
    total = near[...] + jnp.concatenate([left[...], right[...]], axis=1).astype(F32)
    half = total.shape[1]
    size = half // 2
    placing = placing_t[:, :CAP]
    copies = []
    for step in range(4):
        rows = slice(0, CAP) if step < 2 else slice(CAP, BLOCK)
        at = (step % 2) * size
        columns = slice(step * size, (step + 1) * size)
        tile[:, columns] = mul(placing, total[rows, at : at + size].astype(BF16)).astype(BF16)
        copies.append(pltpu.make_async_copy(tile.at[:, columns], grad_in.at[:, columns], done.at[step]))
        copies[-1].start()
    for copy in copies:
        copy.wait()


def grads_kernel(*refs):
    blocks, hiddens, d_pres, outs, tiles, done = refs[:8], refs[8:12], refs[12:16], refs[16:19], refs[19:22], refs[22]
    features, width = outs[0].shape
    size = features // 4

    def groups(values):
        return jnp.concatenate(
            [v[: 2 * MAIN, :] for v in values] + [v[2 * MAIN :, :] for v in values], axis=0
        )

    d_pre, hidden = groups(d_pres), groups(hiddens)
    copies = []
    for step in range(4):
        at = slice(step * size, (step + 1) * size)
        x = rows_of(blocks, 0, False, at)
        tiles[0][at, :] = mul(x, d_pre[:, :width], 0, 0).astype(BF16)
        tiles[1][at, :] = mul(x, d_pre[:, width:], 0, 0).astype(BF16)
        tiles[2][:, at] = mul(hidden, rows_of(blocks, MAIN, True, at), 0, 0).astype(BF16)
        for i, place in enumerate(((at, slice(None)), (at, slice(None)), (slice(None), at))):
            copy = pltpu.make_async_copy(tiles[i].at[place], outs[i].at[place], done.at[3 * step + i])
            copy.start()
            copies.append(copy)
    for copy in copies:
        copy.wait()


def load_kernel(*refs):
    copies = [pltpu.make_async_copy(refs[i], refs[3 + i], refs[6].at[i]) for i in range(3)]
    for copy in copies:
        copy.start()
    for copy in copies:
        copy.wait()


def four_by_two(tokens, grad_out, expert_ids, gate_probs, w_gate, w_up, w_down):
    features, width = w_gate.shape
    half = features // 2
    in_hbm = pl.BlockSpec(memory_space=pltpu.HBM)

    def across(value):
        return lax.ppermute(value, "expert", [(i, i ^ 1) for i in range(8)])

    def along(value, distance):
        return lax.ppermute(value, "expert", [(i, i ^ (2 * distance)) for i in range(8)])

    def after(value, *others):
        return lax.optimization_barrier((value,) + others)[0]

    def hbm(value):
        return pltpu.with_memory_space_constraint(value, pltpu.HBM)

    own, placing_t = call(
        place_kernel,
        (
            struct(BLOCK, features, BF16),
            struct(tokens.shape[0], tokens.shape[0], BF16),
        ),
        hbm(tokens), hbm(grad_out), hbm(expert_ids.T), hbm(gate_probs.T), name="place",
        in_specs=[in_hbm] * 4,
        scratch_shapes=[
            pltpu.VMEM(tokens.shape, BF16),
            pltpu.VMEM(tokens.shape, BF16),
            pltpu.VMEM(expert_ids.shape[::-1], jnp.int32),
            pltpu.VMEM(gate_probs.shape[::-1], F32),
            pltpu.SemaphoreType.DMA((4,)),
        ],
    )
    w_gate, w_up, w_down, _ = lax.optimization_barrier((w_gate, w_up, w_down, own))
    gate, up, down = call(
        load_kernel,
        tuple(struct(*w.shape, BF16) for w in (w_gate, w_up, w_down)),
        hbm(w_gate), hbm(w_up), hbm(w_down), name="load",
        in_specs=[in_hbm] * 3,
        scratch_shapes=[pltpu.SemaphoreType.DMA((3,))],
    )

    def front(mine, other):
        part, sent = call(
            front_kernel,
            (struct(GROUP, 3 * width, F32), struct(GROUP, 3 * width, BF16)),
            mine, other, gate, up, down, name="front",
        )
        return part, lax.ppermute(sent, "tensor", [(0, 1), (1, 0)])

    def back(part, arrived, *pieces):
        return call(
            back_kernel,
            (struct(GROUP, width, BF16), struct(GROUP, 2 * width, BF16), struct(BLOCK, half, F32))
            + tuple(struct(BLOCK, size, BF16) for size in pieces or (half,)),
            part, arrived, gate, up, name="back",
        )

    def add(term, sent):
        return call(add_kernel, struct(BLOCK, half, BF16), term, across(sent), name="add")

    def middle(value):
        return lax.ppermute(value, "expert", [(2, 4), (3, 5), (4, 2), (5, 3)])

    def ends(value):
        return lax.ppermute(value, "expert", [(4, 6), (5, 7), (2, 0), (3, 1)])

    def relay(value):
        pairs = [(0, 2), (1, 3), (2, 6), (3, 7), (4, 0), (5, 1), (6, 4), (7, 5)]
        return lax.ppermute(value, "expert", pairs)

    own_y = across(own)
    two = along(own, 2)
    one = along(own, 1)
    h0, d0, t0, s0 = back(*front(own, own_y))
    one_y = along(own_y, 1)
    pair = call(pair_kernel, struct(BLOCK, 2 * features, BF16), own, own_y, name="pair")
    q0 = add(t0, s0)
    two, one, q0, pair = lax.optimization_barrier((two, one, q0, pair))
    inner = middle(after(pair, two))
    outer = ends(two)
    two_y = across(two)
    h1, d1, t1, s1 = back(*front(one, one_y))
    q1 = add(t1, s1)
    two_y, s1 = lax.optimization_barrier((two_y, s1))
    outer_y = ends(two_y)
    part2, swap2 = front(two, two_y)
    h2, d2, t2, s2 = back(after(part2, outer, q1), swap2)
    q2 = add(t2, s2)
    got = relay(q2)
    large = half * 2 // 3
    three, three_y = call(
        split_kernel, (struct(BLOCK, features, BF16),) * 2, inner, outer, outer_y, name="split"
    )
    h3, d3, t3, *s3 = back(*front(three, three_y), large, half - large)
    r1 = along(after(q1, *s3), 1)
    q3 = [
        call(
            functools.partial(last_kernel, at), struct(*value.shape, BF16),
            t3, across(value), got, name="last",
        )
        for at, value in zip((0, large), s3)
    ]
    r3 = [along(value, 3) for value in q3]

    grads = call(
        grads_kernel,
        (struct(features, width, BF16), struct(features, width, BF16), struct(width, features, BF16)),
        after(own, q3[1]), own_y, one, one_y, two, two_y, three, three_y, h0, h1, h2, h3, d0, d1, d2, d3,
        name="grads",
        out_specs=(pl.BlockSpec(memory_space=pltpu.HBM),) * 3,
        scratch_shapes=[
            pltpu.VMEM(w_gate.shape, BF16),
            pltpu.VMEM(w_up.shape, BF16),
            pltpu.VMEM(w_down.shape, BF16),
            pltpu.SemaphoreType.DMA((12,)),
        ],
    )
    grads, r1 = lax.optimization_barrier((grads, r1))
    near = call(near_kernel, struct(BLOCK, half, F32), q0, r1, got, name="near")
    grad_in = call(
        finish_kernel, struct(tokens.shape[0], features, BF16), placing_t, near, *after(r3, near), name="finish",
        out_specs=in_hbm,
        scratch_shapes=[pltpu.VMEM(tokens.shape, BF16), pltpu.SemaphoreType.DMA((4,))],
    )
    return (grad_in,) + tuple(grads)


def solution(mesh):
    in_specs = (
        P(("pipe", "expert"), "tensor"),
        P(("pipe", "expert"), "tensor"),
        P(("pipe", "expert"), None),
        P(("pipe", "expert"), None),
        P("tensor", "expert"),
        P("tensor", "expert"),
        P("expert", "tensor"),
    )
    out_specs = (
        P(("pipe", "expert"), "tensor"),
        P(("pipe", "tensor"), "expert"),
        P(("pipe", "tensor"), "expert"),
        P(("pipe", "expert"), "tensor"),
    )
    small = mesh.shape["expert"] == 8 and mesh.shape["tensor"] == 2
    body = four_by_two if small else any_size
    return jax.shard_map(body, mesh=mesh, in_specs=in_specs, out_specs=out_specs, check_vma=False)
```

```python
import functools

import jax
import jax.numpy as jnp
from jax import lax
from jax.experimental import pallas as pl
from jax.experimental.pallas import tpu as pltpu
from jax.sharding import PartitionSpec as P

CAP = 36


window_expert = 0


def swiglu_grads(sums, width):
    z_gate = sums[:, :width]
    z_up = sums[:, width : 2 * width]
    d_hidden = sums[:, 2 * width :]
    sig = jax.nn.sigmoid(z_gate)
    act = z_gate * sig
    hidden = (act * z_up).astype(jnp.bfloat16)
    d_gate = (d_hidden * z_up * sig * (1.0 + z_gate * (1.0 - sig))).astype(jnp.bfloat16)
    d_up = (d_hidden * act).astype(jnp.bfloat16)
    return (hidden, jnp.concatenate([d_gate, d_up], axis=1))


def place(tokens, grad_out, expert_ids, gate_probs):
    chosen = expert_ids == window_expert
    weight = jnp.sum(jnp.where(chosen, gate_probs, jnp.zeros_like(gate_probs)), axis=1)
    scaled = (weight[:, None] * grad_out.astype(jnp.float32)).astype(jnp.bfloat16)
    routed = jnp.any(chosen, axis=1)
    slot_of = jnp.cumsum(routed.astype(jnp.int32)) - 1
    slot_ids = jnp.arange(CAP, dtype=jnp.int32)
    placing = ((slot_of[None, :] == slot_ids[:, None]) & routed[None, :]).astype(jnp.bfloat16)
    send_x = jnp.dot(placing, tokens, preferred_element_type=jnp.float32).astype(jnp.bfloat16)
    send_dy = jnp.dot(placing, scaled, preferred_element_type=jnp.float32).astype(jnp.bfloat16)
    return placing, send_x, send_dy


def unplace(placing, summed):
    return lax.dot_general(
        placing, summed, (((0,), (0,)), ((), ())), preferred_element_type=jnp.float32
    ).astype(jnp.bfloat16)


def weight_grads(rows_x, rows_dy, hidden, d_pre, width):
    grad_w_in = lax.dot_general(
        rows_x, d_pre, (((0,), (0,)), ((), ())), preferred_element_type=jnp.float32
    ).astype(jnp.bfloat16)
    grad_down = lax.dot_general(
        hidden, rows_dy, (((0,), (0,)), ((), ())), preferred_element_type=jnp.float32
    ).astype(jnp.bfloat16)
    return (grad_w_in[:, :width], grad_w_in[:, width:], grad_down)


def any_size(tokens, grad_out, expert_ids, gate_probs, w_gate, w_up, w_down):
    width = w_gate.shape[1]
    placing, send_x, send_dy = place(tokens, grad_out, expert_ids, gate_probs)
    rows_x, rows_dy = (
        lax.all_gather(send_x, "expert", axis=0, tiled=True),
        lax.all_gather(send_dy, "expert", axis=0, tiled=True),
    )
    w_in = jnp.concatenate([w_gate, w_up], axis=1)
    front = jnp.dot(rows_x, w_in, preferred_element_type=jnp.float32)
    back = lax.dot_general(
        rows_dy, w_down, (((1,), (1,)), ((), ())), preferred_element_type=jnp.float32
    )
    partial_value = jnp.concatenate([front, back], axis=1)
    share = lax.psum_scatter(
        partial_value.astype(jnp.bfloat16), "tensor", scatter_dimension=0, tiled=True
    ).astype(jnp.float32)
    hidden_part, grads_part = swiglu_grads(share, width)
    hidden, d_pre = (
        lax.all_gather(hidden_part, "tensor", axis=0, tiled=True),
        lax.all_gather(grads_part, "tensor", axis=0, tiled=True),
    )
    summed = lax.psum_scatter(
        lax.dot_general(
            d_pre, w_in, (((1,), (1,)), ((), ())), preferred_element_type=jnp.float32
        ).astype(jnp.bfloat16),
        "expert",
        scatter_dimension=0,
        tiled=True,
    )
    grad_in = unplace(placing, summed)
    return (grad_in,) + weight_grads(rows_x, rows_dy, hidden, d_pre, width)


MAIN = 32
TAIL = CAP - MAIN
BLOCK = 2 * CAP
TERM = 40
GROUP = 80
BF16, F32 = jnp.bfloat16, jnp.float32


def struct(rows, columns, dtype):
    return jax.ShapeDtypeStruct((rows, columns), dtype)


def call(kernel, outs, *args, name, **more):
    return pl.pallas_call(
        kernel,
        out_shape=outs,
        name=name,
        compiler_params=pltpu.CompilerParams(vmem_limit_bytes=24 * 2**20),
        cost_estimate=pl.CostEstimate(flops=1000, bytes_accessed=1000, transcendentals=0),
        **more,
    )(*args)


def mul(left, right, left_dim=1, right_dim=0):
    return lax.dot_general(
        left, right, (((left_dim,), (right_dim,)), ((), ())), preferred_element_type=F32
    )


def place_kernel(
    tokens_at, grad_out_at, ids_at, probs_at, block, placing_t, tokens, grad_out, ids, probs, done
):
    half = tokens.shape[1] // 2
    parts = (slice(0, half), slice(half, 2 * half))
    pairs = [(ids_at, ids), (probs_at, probs)]
    for columns in parts:
        pairs += [(tokens_at.at[:, columns], tokens.at[:, columns])]
        pairs += [(grad_out_at.at[:, columns], grad_out.at[:, columns])]
    copies = [pltpu.make_async_copy(a, b, done.at[i]) for i, (a, b) in enumerate(pairs)]
    for copy in copies:
        copy.start()
    rows = tokens.shape[0]
    copies[0].wait()
    copies[1].wait()
    chosen = ids[...] == window_expert
    weight_row = jnp.sum(jnp.where(chosen, probs[...], 0.0), axis=0, keepdims=True)
    routed_row = jnp.max(chosen.astype(F32), axis=0, keepdims=True)
    at_row = lax.broadcasted_iota(jnp.int32, (rows, rows), 0)
    at_column = lax.broadcasted_iota(jnp.int32, (rows, rows), 1)
    same = at_row == at_column
    routed = jnp.sum(jnp.where(same, routed_row, 0.0), axis=1, keepdims=True)
    slot_row = jnp.sum(jnp.where(at_row <= at_column, routed, 0.0), axis=0, keepdims=True) - 1.0
    slot = jnp.sum(jnp.where(at_column <= at_row, routed_row, 0.0), axis=1, keepdims=True) - 1.0
    wanted = lax.broadcasted_iota(jnp.int32, (TERM, rows), 0).astype(F32)
    placing = jnp.where((slot_row == wanted) & (routed_row > 0.0), 1.0, 0.0)
    wanted = at_column.astype(F32)
    placing_t[...] = jnp.where((slot == wanted) & (routed > 0.0), 1.0, 0.0).astype(BF16)
    scale = jnp.sum(placing * weight_row, axis=1, keepdims=True)
    placing = placing.astype(BF16)
    for step, columns in enumerate(parts):
        copies[2 * step + 2].wait()
        x = mul(placing, tokens[:, columns])
        copies[2 * step + 3].wait()
        dy = mul(placing, grad_out[:, columns]) * scale
        last = jnp.concatenate([x[MAIN:CAP], dy[MAIN:CAP]], axis=0)
        for at, value in ((0, x[0:MAIN]), (MAIN, dy[0:MAIN]), (2 * MAIN, last)):
            block[at : at + value.shape[0], columns] = value.astype(BF16)


def tails(blocks, turned, columns):
    parts = []
    for block in blocks:
        last = block[2 * MAIN : BLOCK, columns].astype(F32)
        if turned:
            last = jnp.concatenate([last[TAIL:], last[:TAIL]], axis=0)
        parts.append(last)
    return jnp.concatenate(parts, axis=0).astype(BF16)


def rows_of(blocks, first, turned, columns):
    main = [block[first : first + MAIN, columns] for block in blocks]
    last = [tails(blocks[i : i + 2], turned, columns) for i in range(0, len(blocks), 2)]
    return jnp.concatenate(main + last, axis=0)


def front_kernel(mine, other, w_gate, w_up, w_down, part, sent):
    width = w_gate.shape[1]
    x = rows_of((mine, other), 0, False, slice(None))
    dy = rows_of((mine, other), MAIN, True, slice(None))
    for at, value in enumerate((mul(x, w_gate[...]), mul(x, w_up[...]), mul(dy, w_down[...], 1, 1))):
        part[:, at * width : (at + 1) * width] = value
        sent[:, at * width : (at + 1) * width] = value.astype(BF16)


def folded(main, last):
    half = main.shape[1] // 2
    return jnp.concatenate([main[:, :half], last[:, :half], main[:, half:], last[:, half:]], axis=0)


def back_kernel(part, arrived, w_gate, w_up, hidden, d_pre, term, *sent):
    width = w_gate.shape[1]
    sums = part[...] + arrived[...].astype(F32)
    z_gate, z_up, d_hidden = (sums[:, i * width : (i + 1) * width] for i in range(3))
    sig = jax.nn.sigmoid(z_gate)
    act = z_gate * sig
    row = lax.broadcasted_iota(jnp.int32, (GROUP, width), 0)
    real = (row < 2 * MAIN) | (row % 8 < TAIL)
    hidden[...] = jnp.where(real, act * z_up, 0.0).astype(BF16)
    d_gate = d_hidden * z_up * sig * (1.0 + z_gate * (1.0 - sig))
    d_gate = jnp.where(real, d_gate, 0.0).astype(BF16)
    d_up = jnp.where(real, d_hidden * act, 0.0).astype(BF16)
    d_pre[:, :width] = d_gate
    d_pre[:, width:] = d_up
    value = mul(d_gate, w_gate[...], 1, 1) + mul(d_up, w_up[...], 1, 1)
    term[...] = folded(value[0:MAIN], value[2 * MAIN : 2 * MAIN + TAIL])
    other = folded(value[MAIN : 2 * MAIN], value[2 * MAIN + 8 : 2 * MAIN + 8 + TAIL]).astype(BF16)
    at = 0
    for piece in sent:
        piece[...] = other[:, at : at + piece.shape[1]]
        at += piece.shape[1]


def pair_kernel(left, right, out):
    width = left.shape[1]
    out[:, :width] = left[...]
    out[:, width:] = right[...]


def split_kernel(inner, outer, outer_y, block, block_y):
    width = block.shape[1]
    block[...] = inner[:, :width] + outer[...]
    block_y[...] = inner[:, width:] + outer_y[...]


def add_kernel(term, arrived, total):
    total[...] = (term[...] + arrived[...].astype(F32)).astype(BF16)


def is_inner():
    line = lax.axis_index("expert") // 2
    return (line == 1) | (line == 2)


def last_kernel(start, term, arrived, passed, total):
    columns = slice(start, start + total.shape[1])
    value = term[:, columns] + arrived[...].astype(F32)
    total[...] = jnp.where(is_inner(), value + passed[:, columns].astype(F32), value).astype(BF16)


def near_kernel(first, second, passed, total):
    value = first[...].astype(F32) + second[...].astype(F32)
    total[...] = jnp.where(is_inner(), value, value + passed[...].astype(F32))


def finish_kernel(placing_t, near, left, right, grad_in, tile, done):
    total = near[...] + jnp.concatenate([left[...], right[...]], axis=1).astype(F32)
    half = total.shape[1]
    size = half // 2
    placing = placing_t[:, :CAP]
    copies = []
    for step in range(4):
        rows = slice(0, CAP) if step < 2 else slice(CAP, BLOCK)
        at = (step % 2) * size
        columns = slice(step * size, (step + 1) * size)
        tile[:, columns] = mul(placing, total[rows, at : at + size].astype(BF16)).astype(BF16)
        copies.append(pltpu.make_async_copy(tile.at[:, columns], grad_in.at[:, columns], done.at[step]))
        copies[-1].start()
    for copy in copies:
        copy.wait()


def grads_kernel(*refs):
    blocks, hiddens, d_pres, outs, tiles, done = refs[:8], refs[8:12], refs[12:16], refs[16:19], refs[19:22], refs[22]
    features, width = outs[0].shape
    size = features // 4

    def groups(values):
        return jnp.concatenate(
            [v[: 2 * MAIN, :] for v in values] + [v[2 * MAIN :, :] for v in values], axis=0
        )

    d_pre, hidden = groups(d_pres), groups(hiddens)
    copies = []
    for step in range(4):
        at = slice(step * size, (step + 1) * size)
        x = rows_of(blocks, 0, False, at)
        tiles[0][at, :] = mul(x, d_pre[:, :width], 0, 0).astype(BF16)
        tiles[1][at, :] = mul(x, d_pre[:, width:], 0, 0).astype(BF16)
        tiles[2][:, at] = mul(hidden, rows_of(blocks, MAIN, True, at), 0, 0).astype(BF16)
        for i, place in enumerate(((at, slice(None)), (at, slice(None)), (slice(None), at))):
            copy = pltpu.make_async_copy(tiles[i].at[place], outs[i].at[place], done.at[3 * step + i])
            copy.start()
            copies.append(copy)
    for copy in copies:
        copy.wait()


def load_kernel(*refs):
    copies = [pltpu.make_async_copy(refs[i], refs[3 + i], refs[6].at[i]) for i in range(3)]
    for copy in copies:
        copy.start()
    for copy in copies:
        copy.wait()


def four_by_two(tokens, grad_out, expert_ids, gate_probs, w_gate, w_up, w_down):
    features, width = w_gate.shape
    half = features // 2
    in_hbm = pl.BlockSpec(memory_space=pltpu.HBM)

    def across(value):
        return lax.ppermute(value, "expert", [(i, i ^ 1) for i in range(8)])

    def along(value, distance):
        return lax.ppermute(value, "expert", [(i, i ^ (2 * distance)) for i in range(8)])

    def after(value, *others):
        return lax.optimization_barrier((value,) + others)[0]

    def hbm(value):
        return pltpu.with_memory_space_constraint(value, pltpu.HBM)

    own, placing_t = call(
        place_kernel,
        (
            struct(BLOCK, features, BF16),
            struct(tokens.shape[0], tokens.shape[0], BF16),
        ),
        hbm(tokens), hbm(grad_out), hbm(expert_ids.T), hbm(gate_probs.T), name="place",
        in_specs=[in_hbm] * 4,
        scratch_shapes=[
            pltpu.VMEM(tokens.shape, BF16),
            pltpu.VMEM(tokens.shape, BF16),
            pltpu.VMEM(expert_ids.shape[::-1], jnp.int32),
            pltpu.VMEM(gate_probs.shape[::-1], F32),
            pltpu.SemaphoreType.DMA((6,)),
        ],
    )
    w_gate, w_up, w_down, _ = lax.optimization_barrier((w_gate, w_up, w_down, own))
    gate, up, down = call(
        load_kernel,
        tuple(struct(*w.shape, BF16) for w in (w_gate, w_up, w_down)),
        hbm(w_gate), hbm(w_up), hbm(w_down), name="load",
        in_specs=[in_hbm] * 3,
        scratch_shapes=[pltpu.SemaphoreType.DMA((3,))],
    )

    def front(mine, other):
        part, sent = call(
            front_kernel,
            (struct(GROUP, 3 * width, F32), struct(GROUP, 3 * width, BF16)),
            mine, other, gate, up, down, name="front",
        )
        return part, lax.ppermute(sent, "tensor", [(0, 1), (1, 0)])

    def back(part, arrived, *pieces):
        return call(
            back_kernel,
            (struct(GROUP, width, BF16), struct(GROUP, 2 * width, BF16), struct(BLOCK, half, F32))
            + tuple(struct(BLOCK, size, BF16) for size in pieces or (half,)),
            part, arrived, gate, up, name="back",
        )

    def add(term, sent):
        return call(add_kernel, struct(BLOCK, half, BF16), term, across(sent), name="add")

    def middle(value):
        return lax.ppermute(value, "expert", [(2, 4), (3, 5), (4, 2), (5, 3)])

    def ends(value):
        return lax.ppermute(value, "expert", [(4, 6), (5, 7), (2, 0), (3, 1)])

    def relay(value):
        pairs = [(0, 2), (1, 3), (2, 6), (3, 7), (4, 0), (5, 1), (6, 4), (7, 5)]
        return lax.ppermute(value, "expert", pairs)

    own_y = across(own)
    two = along(own, 2)
    one = along(own, 1)
    h0, d0, t0, s0 = back(*front(own, own_y))
    one_y = along(own_y, 1)
    pair = call(pair_kernel, struct(BLOCK, 2 * features, BF16), own, own_y, name="pair")
    q0 = add(t0, s0)
    two, one, q0, pair = lax.optimization_barrier((two, one, q0, pair))
    inner = middle(after(pair, two))
    outer = ends(two)
    two_y = across(two)
    h1, d1, t1, s1 = back(*front(one, one_y))
    q1 = add(t1, s1)
    two_y, s1 = lax.optimization_barrier((two_y, s1))
    outer_y = ends(two_y)
    part2, swap2 = front(two, two_y)
    h2, d2, t2, s2 = back(after(part2, outer, q1), swap2)
    q2 = add(t2, s2)
    got = relay(q2)
    large = half * 2 // 3
    three, three_y = call(
        split_kernel, (struct(BLOCK, features, BF16),) * 2, inner, outer, outer_y, name="split"
    )
    h3, d3, t3, *s3 = back(*front(three, three_y), large, half - large)
    r1 = along(after(q1, *s3), 1)
    q3 = [
        call(
            functools.partial(last_kernel, at), struct(*value.shape, BF16),
            t3, across(value), got, name="last",
        )
        for at, value in zip((0, large), s3)
    ]
    r3 = [along(value, 3) for value in q3]

    grads = call(
        grads_kernel,
        (struct(features, width, BF16), struct(features, width, BF16), struct(width, features, BF16)),
        after(own, q3[1]), own_y, one, one_y, two, two_y, three, three_y, h0, h1, h2, h3, d0, d1, d2, d3,
        name="grads",
        out_specs=(pl.BlockSpec(memory_space=pltpu.HBM),) * 3,
        scratch_shapes=[
            pltpu.VMEM(w_gate.shape, BF16),
            pltpu.VMEM(w_up.shape, BF16),
            pltpu.VMEM(w_down.shape, BF16),
            pltpu.SemaphoreType.DMA((12,)),
        ],
    )
    grads, r1 = lax.optimization_barrier((grads, r1))
    near = call(near_kernel, struct(BLOCK, half, F32), q0, r1, got, name="near")
    grad_in = call(
        finish_kernel, struct(tokens.shape[0], features, BF16), placing_t, near, *after(r3, near), name="finish",
        out_specs=in_hbm,
        scratch_shapes=[pltpu.VMEM(tokens.shape, BF16), pltpu.SemaphoreType.DMA((4,))],
    )
    return (grad_in,) + tuple(grads)


def solution(mesh):
    in_specs = (
        P(("pipe", "expert"), "tensor"),
        P(("pipe", "expert"), "tensor"),
        P(("pipe", "expert"), None),
        P(("pipe", "expert"), None),
        P("tensor", "expert"),
        P("tensor", "expert"),
        P("expert", "tensor"),
    )
    out_specs = (
        P(("pipe", "expert"), "tensor"),
        P(("pipe", "tensor"), "expert"),
        P(("pipe", "tensor"), "expert"),
        P(("pipe", "expert"), "tensor"),
    )
    small = mesh.shape["expert"] == 8 and mesh.shape["tensor"] == 2
    body = four_by_two if small else any_size
    return jax.shard_map(body, mesh=mesh, in_specs=in_specs, out_specs=out_specs, check_vma=False)
```
